256 devices in a mesh: grp: 2 (over y_lo), row: 16 (over z, core), col: 8 (over y_hi, x).
Axes of the slice: x: 4, y: 4 (y_hi: 2, y_lo: 2; y = y_hi * 2 + y_lo), z: 8, core: 2. Of those that a mesh axis runs over, the one named last changes fastest.
Arguments:
- pair: float32 [2, 512, 512, 128], P('grp', 'row', 'col'), may hold values from -6 to 6
- pair_mask: int32 [2, 512], P('grp'), may hold values from 0 to 1, as said below
- prev_pair: float32 [2, 512, 512, 128], P('grp', 'row', 'col'), may hold values from -70 to 70
- diff_tokens: float32 [2, 32, 512, 768], P('grp', 'row', 'col'), may hold values from -6 to 6
- diff_mask: int32 [2, 512], P('grp'), may hold values from 0 to 1, as said below
- atom_feats: bfloat16 [2, 32, 2048, 128], P('grp', 'row', 'col'), may hold values from -6 to 6
- atom_token: int32 [2, 2048], P('grp', 'col'), may hold values from 0 to 511, as said below
- trunk_in: bfloat16 [2, 128, 640], replicated, may hold values from -0.5 to 0.5
- trunk_out: bfloat16 [2, 128, 128], replicated, may hold values from -0.5 to 0.5
- bias_weight: bfloat16 [128, 16], replicated, may hold values from -1000 to 1000
- atom_weight: bfloat16 [128, 768], replicated, may hold values from -0.5 to 0.5
- attn_in: bfloat16 [768, 3072], replicated, may hold values from -0.21875 to 0.21875
- attn_out: bfloat16 [768, 768], replicated, may hold values from -0.21875 to 0.21875
Outputs:
- pair_next: float32 [2, 512, 512, 128], P('grp', 'row', 'col')
- tokens_next: float32 [2, 32, 512, 768], P('grp', 'row', 'col')
The draws below stay inside these ranges and needn't reach their ends.
Inputs may be any that keep to these rules, and one draw needn't show every extreme that they name: `pair_mask`: each complex's first tokens are 1 and the rest 0; the first token is always 1 and the last always 0. `diff_mask`: each complex's first tokens are 1 and the rest 0; the first token is always 1 and the last always 0. `atom_token`: atoms b * 256 to (b + 1) * 256 - 1 belong to tokens b * 64 to (b + 1) * 64 - 1, and every token has at least one atom.
All inputs are finite; a program needn't handle non-finite values.
Results may differ from the reference program's by a relative error of at most 0.015.
Values may be sent and summed in bfloat16 or wider, within the bound.
No kernel may reach another device: no remote copies, remote signals or barrier semaphores. Data moves between devices by JAX's collectives and lax.ppermute only.
A program may use at most 128 MiB of HBM per device.

```python
import math
import jax
import jax.numpy as jnp
from jax import lax

C = 128
CA = 128
D = 768
H = 16
TOKENS = 512
TOK_COL = 64
SAMPLES = 32
ATOM_DEV = 256
ATOMS = 2048
N_GRP = 2
N_ROW = 16
N_COL = 8


def padded_mask(key):
    lengths = jax.random.randint(key, (2,), TOKENS // 2, TOKENS)
    return (jnp.arange(TOKENS, dtype=jnp.int32)[None, :] < lengths[:, None]).astype(jnp.int32)


def sign_pattern():
    signs = 1.0 - 2.0 * (jnp.arange(C, dtype=jnp.int32) % 2).astype(jnp.float32)
    return signs


def draw_pair_mask(key, part):
    key = jax.random.fold_in(key, 1)
    return padded_mask(key)


def draw_diff_mask(key, part):
    key = jax.random.fold_in(key, 2)
    return padded_mask(key)


def draw_atom_token(key, part):
    key = jax.random.fold_in(key, 3)
    blocks = ATOMS // ATOM_DEV
    spare = jax.random.randint(key, (2, blocks, ATOM_DEV - TOK_COL), 0, TOK_COL)
    firsts = jnp.broadcast_to(jnp.arange(TOK_COL, dtype=jnp.int32)[None, None, :], (2, blocks, TOK_COL))
    within = jnp.concatenate([firsts, spare.astype(jnp.int32)], axis=2)
    offsets = (jnp.arange(blocks, dtype=jnp.int32) * TOK_COL)[None, :, None]
    return (within + offsets).reshape(2, ATOMS).astype(jnp.int32)


def draw_bias_weight(key, part):
    key = jax.random.fold_in(key, 4)
    first_key = jax.random.fold_in(key, 0)
    third_key = jax.random.fold_in(key, 2)
    fourth_key = jax.random.fold_in(key, 3)
    base = jax.random.normal(first_key, (C, H), jnp.float32) * C ** (-0.5)
    order = jax.random.permutation(third_key, H)
    chosen = (order < max(1, H // 4)).astype(jnp.float32)
    beta = jax.random.uniform(fourth_key, (H,), jnp.float32, 120.0, 300.0) * chosen
    return (base + sign_pattern()[:, None] * beta[None, :] / C).astype(jnp.bfloat16)


def draw_prev_pair(key, part):
    key = jax.random.fold_in(key, 5)
    first_key, second_key, third_key = jax.random.split(key, 3)
    noise = jnp.clip(jax.random.normal(first_key, (2, TOKENS, TOKENS, C), jnp.float32), -6.0, 6.0)
    picks = jax.random.randint(second_key, (2, TOKENS), 0, 8)
    first_row = (jnp.arange(TOKENS, dtype=jnp.int32) == 0)[None, :]
    shifted = jnp.logical_or(picks == 0, first_row).astype(jnp.float32)
    amount = jnp.exp(jax.random.uniform(third_key, (2, TOKENS), jnp.float32, math.log(20.0), math.log(60.0))) * shifted
    return noise + amount[:, :, None, None] * sign_pattern()[None, None, None, :]


def steps_of(rng, shape, shards, low, largest):
    gain, own = 1.0, jax.random.fold_in(rng, 6)
    for dim, shards_of in shards:
        heights = jnp.exp(jax.random.uniform(jax.random.fold_in(own, dim), (shards_of,), jnp.float32, low / len(shards), largest / len(shards)))
        gain = gain * jnp.repeat(heights, shape[dim] // shards_of).reshape([-1 if axis == dim else 1 for axis in range(len(shape))])
    return gain


def normal_values(stream_key, dims, scale, bound, cuts=(), kind=jnp.bfloat16):
    result = scale * jax.random.normal(stream_key, dims, jnp.float32)
    if cuts:
        result = result * steps_of(stream_key, dims, cuts, -0.22, 0.18)
    return jnp.clip(result, -bound, bound).astype(kind)


def setup_inputs(seed: int = 0) -> dict:
    key_of = jax.random.split(jax.random.key(seed), 14)
    return {
        "pair": normal_values(key_of[0], (N_GRP, TOKENS, TOKENS, C), 1.0, 6.0, ((0, 2), (1, 16), (2, 8)), jnp.float32),
        "pair_mask": draw_pair_mask(jax.random.fold_in(key_of[13], 71), 0),
        "prev_pair": draw_prev_pair(jax.random.fold_in(key_of[13], 71), 0),
        "diff_tokens": normal_values(key_of[3], (N_GRP, SAMPLES, TOKENS, D), 1.0, 6.0, ((0, 2), (1, 16), (2, 8)), jnp.float32),
        "diff_mask": draw_diff_mask(jax.random.fold_in(key_of[13], 71), 0),
        "atom_feats": normal_values(key_of[5], (N_GRP, SAMPLES, ATOMS, CA), 1.0, 6.0, ((0, 2), (1, 16), (2, 8))),
        "atom_token": draw_atom_token(jax.random.fold_in(key_of[13], 71), 0),
        "trunk_in": normal_values(key_of[7], (2, C, 5 * C), C ** -0.5, 0.5),
        "trunk_out": normal_values(key_of[8], (2, C, C), C ** -0.5, 0.5),
        "bias_weight": draw_bias_weight(jax.random.fold_in(key_of[13], 71), 0),
        "atom_weight": normal_values(key_of[10], (CA, D), CA ** -0.5, 0.5),
        "attn_in": normal_values(key_of[11], (D, 4 * D), D ** -0.5, 0.21875),
        "attn_out": normal_values(key_of[12], (D, D), D ** -0.5, 0.21875),
    }


EPSILON = 1e-05

def layer_norm(values):
    centred = values - lax.optimization_barrier(jnp.mean(values, axis=-1, keepdims=True))
    spread = lax.optimization_barrier(jnp.mean(centred * centred, axis=-1, keepdims=True))
    return centred * lax.rsqrt(spread + EPSILON)

def blocked_sum(left_side, right_side, outgoing, blocks):
    left_f = left_side.astype(jnp.float32)
    right_f = right_side.astype(jnp.float32)
    count_tok = left_side.shape[0]
    width = left_side.shape[-1]
    span = count_tok // blocks

    def add_block(total, index):
        first = (index * span).astype(jnp.int32)
        if outgoing:
            left_part = lax.dynamic_slice_in_dim(left_f, first, span, 1)
            right_part = lax.dynamic_slice_in_dim(right_f, first, span, 1)
            term = jnp.einsum('ikc,jkc->ijc', left_part, right_part)
        else:
            left_part = lax.dynamic_slice_in_dim(left_f, first, span, 0)
            right_part = lax.dynamic_slice_in_dim(right_f, first, span, 0)
            term = jnp.einsum('kic,kjc->ijc', left_part, right_part)
        rounded = lax.optimization_barrier(term.astype(jnp.bfloat16))
        return (total + rounded.astype(jnp.float32), None)
    zeros = jnp.zeros((count_tok, count_tok, width), jnp.float32)
    summed, unused = lax.scan(add_block, zeros, jnp.arange(blocks, dtype=jnp.int32))
    return summed

def triangle(pair_in, live, weight_in, weight_out, outgoing, blocks):
    width = pair_in.shape[-1]
    normed = layer_norm(pair_in).astype(jnp.bfloat16)
    projected = jnp.dot(normed, weight_in, preferred_element_type=jnp.float32)
    pair_live = (live[:, None] * live[None, :])[..., None]
    left_side = (pair_live * jax.nn.sigmoid(projected[..., :width]) * projected[..., width:2 * width]).astype(jnp.bfloat16)
    right_side = (pair_live * jax.nn.sigmoid(projected[..., 2 * width:3 * width]) * projected[..., 3 * width:4 * width]).astype(jnp.bfloat16)
    gate_vals = jax.nn.sigmoid(projected[..., 4 * width:])
    summed = blocked_sum(left_side, right_side, outgoing, blocks)
    summed_norm = layer_norm(summed).astype(jnp.bfloat16)
    return pair_in + gate_vals * jnp.dot(summed_norm, weight_out, preferred_element_type=jnp.float32)

def attend_sample(query_one, key_one, value_one, bias_full, key_live, scale):
    scores = jnp.einsum('ihd,jhd->hij', query_one.astype(jnp.float32), key_one.astype(jnp.float32)) * scale + bias_full
    masked = jnp.where(key_live[None, None, :], scores, -1e+30)
    top_val = lax.optimization_barrier(jnp.max(masked, axis=2, keepdims=True))
    weights = jnp.exp(masked - top_val)
    total = lax.optimization_barrier(jnp.sum(weights, axis=2))
    mixed = jnp.einsum('hij,jhd->ihd', weights.astype(jnp.bfloat16).astype(jnp.float32), value_one.astype(jnp.float32))
    return mixed / jnp.transpose(total)[..., None]

def diffuse(tokens_in, token_live, atoms, atom_map, prev_one, bias_weight, atom_weight, attn_in, attn_out):
    samples, count_tok, width = tokens_in.shape
    heads = bias_weight.shape[1]
    head_size = width // heads
    onehot = (atom_map[None, :] == jnp.arange(count_tok, dtype=jnp.int32)[:, None]).astype(jnp.float32)
    atom_count = lax.optimization_barrier(jnp.sum(onehot, axis=1))
    pooled = (jnp.einsum('ta,sac->stc', onehot, atoms.astype(jnp.float32)) / atom_count[None, :, None]).astype(jnp.bfloat16)
    start = tokens_in + jnp.dot(pooled, atom_weight, preferred_element_type=jnp.float32)
    normed = layer_norm(start).astype(jnp.bfloat16)
    projected = jnp.dot(normed, attn_in, preferred_element_type=jnp.float32)
    queries = projected[..., :width].astype(jnp.bfloat16).reshape(samples, count_tok, heads, head_size)
    keys_all = projected[..., width:2 * width].astype(jnp.bfloat16).reshape(samples, count_tok, heads, head_size)
    values_all = projected[..., 2 * width:3 * width].astype(jnp.bfloat16).reshape(samples, count_tok, heads, head_size)
    gate_vals = jax.nn.sigmoid(projected[..., 3 * width:])
    bias_pair = jnp.dot(layer_norm(prev_one).astype(jnp.bfloat16), bias_weight, preferred_element_type=jnp.float32).astype(jnp.bfloat16)
    bias_full = jnp.transpose(bias_pair.astype(jnp.float32), (2, 0, 1))
    key_live = token_live > 0
    scale = head_size ** (-0.5)

    def per_sample(operands):
        return attend_sample(operands[0], operands[1], operands[2], bias_full, key_live, scale)
    mixed = lax.map(per_sample, (queries, keys_all, values_all))
    blended = (gate_vals * mixed.reshape(samples, count_tok, width)).astype(jnp.bfloat16)
    return start + jnp.dot(blended, attn_out, preferred_element_type=jnp.float32)

def reference(pair, pair_mask, prev_pair, diff_tokens, diff_mask, atom_feats, atom_token, trunk_in, trunk_out, bias_weight, atom_weight, attn_in, attn_out):
    pair_outs = []
    token_outs = []
    for group in range(N_GRP):
        live = pair_mask[group].astype(jnp.float32)
        first = triangle(pair[group], live, trunk_in[0], trunk_out[0], True, N_COL)
        pair_outs.append(triangle(first, live, trunk_in[1], trunk_out[1], False, N_ROW))
        token_outs.append(diffuse(diff_tokens[group], diff_mask[group], atom_feats[group], atom_token[group], prev_pair[N_GRP - 1 - group], bias_weight, atom_weight, attn_in, attn_out))
    return (jnp.stack(pair_outs), jnp.stack(token_outs))
```

```python
import functools

import jax
import jax.numpy as jnp
from jax import lax
from jax.experimental import pallas as pl
from jax.experimental.pallas import tpu as pltpu
from jax.sharding import Mesh, PartitionSpec as P

EPSILON = 1e-05
F32, BF16 = jnp.float32, jnp.bfloat16
ROWS, COLS, TOK, C = 32, 64, 512, 128
HEADS, HEAD = 16, 48
VMEM_LIMIT = 48 * 2**20
NT = (((1,), (1,)), ((), ()))
TN = (((0,), (0,)), ((), ()))


def dot(left, right, dims=(((1,), (0,)), ((), ()))):
    return lax.dot_general(left, right, dims, preferred_element_type=F32)


def layer_norm(values, axis=-1):
    centred = values - jnp.mean(values, axis=axis, keepdims=True)
    spread = jnp.mean(centred * centred, axis=axis, keepdims=True)
    return centred * lax.rsqrt(spread + EPSILON)


def low_lanes():
    return lax.broadcasted_iota(jnp.int32, (1, 128), 1) < 64


def swap_halves(first, second):
    low = low_lanes()
    axis = first.ndim - 1
    return (
        jnp.where(low, first, pltpu.roll(second, 64, axis)),
        jnp.where(low, pltpu.roll(first, 64, axis), second),
    )


def pair_step(pair_ref, step):
    return pair_ref[:, step].reshape(2 * COLS, C)


def project_step(values, step, length, row0, col0, weight_ref, spread_ref):
    normed = layer_norm(values).astype(BF16)
    lane = lax.broadcasted_iota(jnp.int32, (1, 128), 1)
    half = (lane >= 64).astype(jnp.int32)
    row = row0 + half * 16 + step
    col = col0 + lane - half * 64
    live = jnp.logical_and(row < length, col < length).astype(F32)
    projected = dot(weight_ref[...], normed, NT)
    left = live * jax.nn.sigmoid(projected[:C]) * projected[C : 2 * C]
    right = live * jax.nn.sigmoid(projected[2 * C : 3 * C]) * projected[3 * C :]
    spread_ref[pl.ds(step, C, stride=32), :] = left
    spread_ref[pl.ds(step + 16, C, stride=32), :] = right


def mask_length(mask_ref):
    return jnp.sum(mask_ref[...])


def project_kernel(place_ref, mask_ref, pair_ref, weight_ref, out_ref, spread_ref):
    length = mask_length(mask_ref)

    def body(step, carry):
        project_step(
            pair_step(pair_ref, step), step, length, place_ref[0], place_ref[1], weight_ref, spread_ref
        )
        return carry

    lax.fori_loop(0, 16, body, 0, unroll=4)
    out_ref[...] = spread_ref[...].astype(BF16).reshape(C, 32, 128)


def gate_kernel(pair_ref, weight_ref, out_ref):
    def body(step, carry):
        normed = layer_norm(pair_step(pair_ref, step)).astype(BF16)
        out_ref[:, step] = jax.nn.sigmoid(dot(normed, weight_ref[...])).reshape(2, COLS, C)
        return carry

    lax.fori_loop(0, 16, body, 0, unroll=4)


def product_kernel(recv_ref, out_ref, left_ref, right_ref, *, outgoing):
    for block in range(4):
        lanes = slice(block * 128, (block + 1) * 128)
        for side, dest_ref in ((0, left_ref), (1, right_ref)):
            rows = slice(side * 16, side * 16 + 16)
            first, second = swap_halves(
                recv_ref[:, 2 * block, rows, :].astype(F32),
                recv_ref[:, 2 * block + 1, rows, :].astype(F32),
            )
            dest_ref[:, 0, :, lanes] = first.astype(BF16)
            dest_ref[:, 1, :, lanes] = second.astype(BF16)
    left = left_ref[...].reshape(TOK, TOK)
    right = right_ref[...].reshape(TOK, TOK)
    for block in range(4):
        lanes = slice(block * 128, (block + 1) * 128)
        if outgoing:
            summed = dot(left, right[lanes], NT)
        else:
            summed = dot(left, right[:, lanes], TN)
        summed = summed.reshape(16, 2, 16, 128)
        first, second = swap_halves(summed[:, 0], summed[:, 1])
        out_ref[:, 2 * block] = first.astype(BF16)
        out_ref[:, 2 * block + 1] = second.astype(BF16)


def finish_step(recv_f32_ref, pair_ref, gate_ref, weight_ref, step):
    summed = recv_f32_ref[pl.ds(step, C, stride=16), :]
    normed = layer_norm(summed, 0).astype(BF16)
    update = dot(normed, weight_ref[...], TN)
    return pair_step(pair_ref, step) + pair_step(gate_ref, step) * update


def finish_project_kernel(
    place_ref, mask_ref, recv_ref, pair_ref, gate_ref, out_weight_ref, in_weight_ref,
    pair_out_ref, out_ref, recv_f32_ref, spread_ref,
):
    length = mask_length(mask_ref)
    recv_f32_ref[...] = recv_ref[...].astype(F32).reshape(C * 16, 128)

    def body(step, carry):
        values = finish_step(recv_f32_ref, pair_ref, gate_ref, out_weight_ref, step)
        pair_out_ref[:, step] = values.reshape(2, COLS, C)
        project_step(values, step, length, place_ref[0], place_ref[1], in_weight_ref, spread_ref)
        return carry

    lax.fori_loop(0, 16, body, 0, unroll=4)
    out_ref[...] = spread_ref[...].astype(BF16).reshape(C, 32, 128)


def finish_kernel(recv_ref, pair_ref, gate_ref, out_weight_ref, pair_out_ref, recv_f32_ref):
    recv_f32_ref[...] = recv_ref[...].astype(F32).reshape(C * 16, 128)

    def body(step, carry):
        values = finish_step(recv_f32_ref, pair_ref, gate_ref, out_weight_ref, step)
        pair_out_ref[:, step] = values.reshape(2, COLS, C)
        return carry

    lax.fori_loop(0, 16, body, 0, unroll=4)


def bias_kernel(prev_ref, weight_ref, out_ref, spread_ref):
    def body(step, carry):
        normed = layer_norm(pair_step(prev_ref, step)).astype(BF16)
        spread_ref[pl.ds(step, HEADS, stride=16), :] = dot(weight_ref[...], normed, NT)
        return carry

    lax.fori_loop(0, 16, body, 0, unroll=4)
    out_ref[...] = spread_ref[...].astype(BF16).reshape(HEADS, 16, 128)


def tokens_kernel(
    place_ref, tokens_ref, atoms_ref, ids_ref, atom_weight_ref, weight_ref, bias_ref,
    start_ref, gate_ref, out_ref,
):
    tokens, atoms = 64, 256
    local = ids_ref[...] - place_ref[1]
    onehot = (lax.broadcasted_iota(jnp.int32, (tokens, atoms), 0) == local).astype(F32)
    count = jnp.sum(onehot, axis=1, keepdims=True)
    onehot = onehot.astype(BF16)
    pooled = [(dot(onehot, atoms_ref[sample]) / count).astype(BF16) for sample in range(2)]
    width = HEADS * HEAD
    start = tokens_ref[...].reshape(128, width) + dot(
        jnp.concatenate(pooled, axis=0), atom_weight_ref[...]
    )
    start_ref[...] = start
    normed = layer_norm(start).astype(BF16)
    for part in range(3):
        projected = dot(normed, weight_ref[:, part * width : (part + 1) * width])
        turned = jnp.transpose(projected, (1, 0)).astype(BF16)
        out_ref[:, part * HEAD : (part + 1) * HEAD, :] = turned.reshape(HEADS, HEAD, 128)
    out_ref[:, 3 * HEAD :, :] = bias_ref[...]
    gate_ref[...] = jax.nn.sigmoid(dot(normed, weight_ref[:, 3 * width :]))


def attention_kernel(mask_ref, recv_ref, bias_ref, out_ref, parts_ref, full_bias_ref, mixed_ref):
    live = lax.broadcasted_iota(jnp.int32, (1, TOK), 1) < mask_length(mask_ref)
    for block in range(4):
        lanes = slice(block * 128, (block + 1) * 128)
        first, second = swap_halves(
            bias_ref[:, 2 * block].astype(F32), bias_ref[:, 2 * block + 1].astype(F32)
        )
        full_bias_ref[:, 0, :, lanes] = first
        full_bias_ref[:, 1, :, lanes] = second
        for core in range(2):
            halves = swap_halves(
                recv_ref[core, 2 * block, : 3 * HEAD, :].astype(F32),
                recv_ref[core, 2 * block + 1, : 3 * HEAD, :].astype(F32),
            )
            for sample in range(2):
                parts_ref[2 * core + sample, : 3 * HEAD, lanes] = halves[sample].astype(BF16)
    parts_ref[:, 3 * HEAD :, :] = jnp.ones((4, 16, TOK), BF16)
    bias = full_bias_ref.reshape(TOK, TOK)

    def body(index, carry):
        query = parts_ref[index, :HEAD, :]
        key = parts_ref[index, HEAD : 2 * HEAD, :]
        value = parts_ref[index, 2 * HEAD :, :]
        scores = dot(query, key, TN) * (HEAD**-0.5) + bias[...]
        scores = jnp.where(live, scores, -1e30)
        top = jnp.max(scores, axis=1, keepdims=True)
        weights = jnp.exp(scores - top).astype(BF16)
        mixed = dot(value, weights, NT)
        mixed_ref[index] = mixed[:HEAD] / mixed[HEAD : HEAD + 1]
        return carry

    lax.fori_loop(0, 4, body, 0)
    for core in range(2):
        for block in range(4):
            lanes = slice(block * 128, (block + 1) * 128)
            first, second = swap_halves(mixed_ref[2 * core, :, lanes], mixed_ref[2 * core + 1, :, lanes])
            out_ref[core, 2 * block] = first.astype(BF16)
            out_ref[core, 2 * block + 1] = second.astype(BF16)


def tokens_out_kernel(recv_ref, gate_ref, start_ref, weight_ref, out_ref):
    width = HEADS * HEAD
    mixed = jnp.transpose(recv_ref[...].reshape(width, 128).astype(F32), (1, 0))
    blended = (gate_ref[...] * mixed).astype(BF16)
    out_ref[...] = (start_ref[...] + dot(blended, weight_ref[...])).reshape(2, 64, width)


def call(kernel, name, out_shape, scratch, *operands, smem=0, flops=10**8):
    shapes = jax.tree.leaves(out_shape)
    nbytes = sum(v.size * v.dtype.itemsize for v in (*operands, *shapes))
    vmem = pl.BlockSpec(memory_space=pltpu.VMEM)
    return pl.pallas_call(
        kernel,
        name=name,
        out_shape=out_shape,
        in_specs=[pl.BlockSpec(memory_space=pltpu.SMEM)] * smem + [vmem] * (len(operands) - smem),
        out_specs=jax.tree.map(lambda _: vmem, out_shape),
        scratch_shapes=scratch,
        cost_estimate=pl.CostEstimate(flops=flops, bytes_accessed=nbytes, transcendentals=0),
        compiler_params=pltpu.CompilerParams(vmem_limit_bytes=VMEM_LIMIT),
    )(*operands)


def shape(*dims, dtype=F32):
    return jax.ShapeDtypeStruct(dims, dtype)


ALL = ("z", "core", "col")
NEAR = ("core", "col")


def exchange(value, axes):
    return lax.all_to_all(value, axes, 0, 0, tiled=True)


def on_device(
    pair, pair_mask, prev_pair, diff_tokens, diff_mask, atom_feats, atom_token,
    trunk_in, trunk_out, bias_weight, atom_weight, attn_in, attn_out,
):
    row = lax.axis_index("z") * 2 + lax.axis_index("core")
    place = jnp.stack([row * ROWS, lax.axis_index("col") * COLS]).astype(jnp.int32)
    tile = (2, 16, COLS, C)
    send = shape(C, 32, 128, dtype=BF16)
    spread = pltpu.VMEM((C * 32, 128), F32)
    received = pltpu.VMEM((C * 16, 128), F32)
    square = pltpu.VMEM((16, 2, 16, TOK), BF16)
    weights = jnp.swapaxes(trunk_in, 1, 2)

    def product(operands, outgoing):
        gathered = exchange(operands, ALL).reshape(16, 8, 32, 128)
        result = call(
            functools.partial(product_kernel, outgoing=outgoing), "product",
            shape(16, 8, 16, 128, dtype=BF16), [square, square], gathered, flops=2 * TOK**3,
        )
        return exchange(result.reshape(C, 16, 128), ALL)

    pair0 = pair.reshape(tile)
    operands = call(
        project_kernel, "project", send, [spread],
        place, pair_mask, pair0, weights[0, : 4 * C], smem=1,
    )
    bias_here = call(
        bias_kernel, "bias", shape(HEADS, 16, 128, dtype=BF16), [pltpu.VMEM((HEADS * 16, 128), F32)],
        prev_pair.reshape(tile), jnp.swapaxes(bias_weight, 0, 1),
    )
    bias_other = lax.ppermute(bias_here, "grp", [(0, 1), (1, 0)])
    gate0 = call(gate_kernel, "gate", shape(*tile), [], pair0, trunk_in[0, :, 4 * C :])
    summed0 = product(operands, True)

    start, gate2, parts = call(
        tokens_kernel, "tokens_in",
        (shape(128, 768), shape(128, 768), shape(HEADS, 160, 128, dtype=BF16)), [],
        place, diff_tokens[0], atom_feats[0], atom_token, atom_weight, attn_in, bias_other, smem=1,
    )
    parts = exchange(parts, NEAR)
    bias_all = lax.all_gather(parts[:, 3 * HEAD :], "z", axis=0, tiled=True)

    pair1, operands = call(
        finish_project_kernel, "finish_project", (shape(*tile), send), [received, spread],
        place, pair_mask, summed0, pair0, gate0, trunk_out[0], weights[1, : 4 * C], smem=1,
    )
    gate1 = call(gate_kernel, "gate", shape(*tile), [], pair1, trunk_in[1, :, 4 * C :])
    summed1 = product(operands, False)

    mixed = call(
        attention_kernel, "attention", shape(2, 8, HEAD, 128, dtype=BF16),
        [
            pltpu.VMEM((4, 160, TOK), BF16),
            pltpu.VMEM((16, 2, 16, TOK), F32),
            pltpu.VMEM((4, HEAD, TOK), F32),
        ],
        diff_mask, parts.reshape(2, 8, 160, 128), bias_all.reshape(16, 8, 16, 128),
    )
    mixed = exchange(mixed.reshape(HEADS, HEAD, 128), NEAR)
    tokens_done = call(
        tokens_out_kernel, "tokens_out", shape(2, 64, 768), [], mixed, gate2, start, attn_out
    )

    pair2 = call(
        finish_kernel, "finish", shape(*tile), [received], summed1, pair1, gate1, trunk_out[1]
    )
    return (pair2.reshape(1, ROWS, COLS, C), tokens_done[None])


def solution(mesh):
    split = Mesh(mesh.devices.reshape(2, 8, 2, 8), ("grp", "z", "core", "col"))
    row = ("z", "core")
    placed = (
        P("grp", row, "col", None),
        P("grp", None),
        P("grp", row, "col", None),
        P("grp", row, "col", None),
        P("grp", None),
        P("grp", row, "col", None),
        P("grp", "col"),
        P(),
        P(),
        P(),
        P(),
        P(),
        P(),
    )
    return jax.shard_map(
        on_device,
        mesh=split,
        in_specs=placed,
        out_specs=(P("grp", row, "col", None), P("grp", row, "col", None)),
        check_vma=False,
    )
```

```python
import functools

import jax
import jax.numpy as jnp
from jax import lax
from jax.experimental import pallas as pl
from jax.experimental.pallas import tpu as pltpu
from jax.sharding import Mesh, PartitionSpec as P

EPSILON = 1e-05
F32, BF16 = jnp.float32, jnp.bfloat16
ROWS, COLS, TOK, C = 32, 64, 512, 128
HEADS, HEAD = 16, 48
WIDTH, PAIR = HEADS * HEAD, 2 * HEAD
VMEM_LIMIT = 48 * 2**20
NT = (((1,), (1,)), ((), ()))
TN = (((0,), (0,)), ((), ()))


def dot(left, right, dims=(((1,), (0,)), ((), ()))):
    return lax.dot_general(left, right, dims, preferred_element_type=F32)


def layer_norm(values, axis=-1):
    centred = values - jnp.mean(values, axis=axis, keepdims=True)
    spread = jnp.mean(centred * centred, axis=axis, keepdims=True)
    return centred * lax.rsqrt(spread + EPSILON)


def low_lanes():
    return lax.broadcasted_iota(jnp.int32, (1, 128), 1) < 64


def swap_halves(first, second):
    low = low_lanes()
    axis = first.ndim - 1
    return (
        jnp.where(low, first, pltpu.roll(second, 64, axis)),
        jnp.where(low, pltpu.roll(first, 64, axis), second),
    )


def pair_step(pair_ref, step):
    return pair_ref[:, step].reshape(2 * COLS, C)


def turned_weight(weight_ref, update):
    return jnp.transpose(weight_ref[update, :, : 4 * C].astype(F32), (1, 0)).astype(BF16)


def project_step(values, step, length, row0, col0, weight, spread_ref):
    normed = layer_norm(values).astype(BF16)
    lane = lax.broadcasted_iota(jnp.int32, (1, 128), 1)
    half = (lane >= 64).astype(jnp.int32)
    row = row0 + half * 16 + step
    col = col0 + lane - half * 64
    live = jnp.logical_and(row < length, col < length).astype(F32)
    projected = dot(weight, normed, NT)
    left = live * jax.nn.sigmoid(projected[:C]) * projected[C : 2 * C]
    right = live * jax.nn.sigmoid(projected[2 * C : 3 * C]) * projected[3 * C :]
    spread_ref[pl.ds(step, C, stride=32), :] = left
    spread_ref[pl.ds(step + 16, C, stride=32), :] = right


def mask_length(mask_ref):
    return jnp.sum(mask_ref[...])


def project_kernel(place_ref, mask_ref, pair_ref, weight_ref, out_ref, spread_ref):
    length = mask_length(mask_ref)
    weight = turned_weight(weight_ref, 0)

    def body(step, carry):
        project_step(
            pair_step(pair_ref, step), step, length, place_ref[0], place_ref[1], weight, spread_ref
        )
        return carry

    lax.fori_loop(0, 16, body, 0, unroll=4)
    out_ref[...] = spread_ref[...].astype(BF16).reshape(C, 32, 128)


def gate_kernel(pair_ref, weight_ref, out_ref, *, update):
    weight = weight_ref[update, :, 4 * C :]

    def body(step, carry):
        normed = layer_norm(pair_step(pair_ref, step)).astype(BF16)
        out_ref[:, step] = jax.nn.sigmoid(dot(normed, weight)).reshape(2, COLS, C)
        return carry

    lax.fori_loop(0, 16, body, 0, unroll=4)


def product_kernel(recv_ref, *refs, outgoing):
    out_ref, left_ref, right_ref = refs[-3:]
    if outgoing:
        bias_ref = refs[0]
        for core in range(2):
            for col in range(8):
                tile = bias_ref[2 * col + core]
                out_ref[core, col, :, 16:, :] = jnp.broadcast_to(tile[None], (8, 16, 128))
    for block in range(4):
        lanes = slice(block * 128, (block + 1) * 128)
        for side, dest_ref in ((0, left_ref), (1, right_ref)):
            rows = slice(side * 16, side * 16 + 16)
            for core in range(2):
                first, second = swap_halves(
                    recv_ref[core, 2 * block, :, rows, :].astype(F32),
                    recv_ref[core, 2 * block + 1, :, rows, :].astype(F32),
                )
                dest_ref[:, core, 0, :, lanes] = first.astype(BF16)
                dest_ref[:, core, 1, :, lanes] = second.astype(BF16)
    left = left_ref[...].reshape(TOK, TOK)
    right = right_ref[...].reshape(TOK, TOK)
    for block in range(4):
        lanes = slice(block * 128, (block + 1) * 128)
        if outgoing:
            summed = dot(left, right[lanes], NT)
        else:
            summed = dot(left, right[:, lanes], TN)
        summed = summed.reshape(8, 2, 2, 16, 128)
        for core in range(2):
            first, second = swap_halves(summed[:, core, 0], summed[:, core, 1])
            out_ref[core, 2 * block, :, :16, :] = first.astype(BF16)
            out_ref[core, 2 * block + 1, :, :16, :] = second.astype(BF16)


def finish_step(recv_f32_ref, pair_ref, gate_ref, weight, step):
    summed = recv_f32_ref[pl.ds(step, C, stride=16), :]
    normed = layer_norm(summed, 0).astype(BF16)
    update = dot(normed, weight, TN)
    return pair_step(pair_ref, step) + pair_step(gate_ref, step) * update


def finish_project_kernel(
    place_ref, mask_ref, recv_ref, pair_ref, gate_ref, out_weight_ref, in_weight_ref,
    pair_out_ref, out_ref, recv_f32_ref, spread_ref,
):
    length = mask_length(mask_ref)
    weight = turned_weight(in_weight_ref, 1)
    recv_f32_ref[...] = recv_ref[:, :16, :].astype(F32).reshape(C * 16, 128)

    def body(step, carry):
        values = finish_step(recv_f32_ref, pair_ref, gate_ref, out_weight_ref[0], step)
        pair_out_ref[:, step] = values.reshape(2, COLS, C)
        project_step(values, step, length, place_ref[0], place_ref[1], weight, spread_ref)
        return carry

    lax.fori_loop(0, 16, body, 0, unroll=4)
    out_ref[...] = spread_ref[...].astype(BF16).reshape(C, 32, 128)


def finish_kernel(recv_ref, pair_ref, gate_ref, out_weight_ref, *refs):
    pair_out_ref, recv_f32_ref = refs[-2:]
    recv_f32_ref[...] = recv_ref[:, :16, :].astype(F32).reshape(C * 16, 128)

    def body(step, carry):
        values = finish_step(recv_f32_ref, pair_ref, gate_ref, out_weight_ref[1], step)
        pair_out_ref[:, step] = values.reshape(2, COLS, C)
        return carry

    lax.fori_loop(0, 16, body, 0, unroll=4)


def bias_kernel(prev_ref, weight_ref, *refs):
    out_ref, spread_ref = refs[-2:]

    def body(step, carry):
        normed = layer_norm(pair_step(prev_ref, step)).astype(BF16)
        spread_ref[pl.ds(step, HEADS, stride=16), :] = dot(weight_ref[...], normed, NT)
        return carry

    lax.fori_loop(0, 16, body, 0, unroll=4)
    out_ref[...] = spread_ref[...].astype(BF16).reshape(HEADS, 16, 128)


def tokens_kernel(
    place_ref, tokens_ref, atoms_ref, ids_ref, atom_weight_ref, weight_ref, *refs,
):
    start_ref, gate_ref, parts_ref = refs[-3:]
    tokens, atoms = 64, 256
    local = ids_ref[...] - place_ref[1]
    onehot = (lax.broadcasted_iota(jnp.int32, (tokens, atoms), 0) == local).astype(F32)
    count = jnp.sum(onehot, axis=1, keepdims=True)
    onehot = onehot.astype(BF16)
    pooled = [(dot(onehot, atoms_ref[sample]) / count).astype(BF16) for sample in range(2)]
    start = tokens_ref[...].reshape(128, WIDTH) + dot(
        jnp.concatenate(pooled, axis=0), atom_weight_ref[...]
    )
    start_ref[...] = start
    normed = layer_norm(start).astype(BF16)
    for part in range(3):
        projected = dot(normed, weight_ref[:, part * WIDTH : (part + 1) * WIDTH])
        turned = jnp.transpose(projected, (1, 0)).astype(BF16)
        parts_ref[:, part * PAIR : (part + 1) * PAIR, :] = turned.reshape(8, PAIR, 128)
    gate_ref[...] = jax.nn.sigmoid(dot(normed, weight_ref[:, 3 * WIDTH :]))


def attention_kernel(place_ref, mask_ref, recv_ref, bias_ref, other_bias_ref, *refs):
    sends = refs[:8]
    query_key_ref, value_ref, full_bias_ref, mixed_ref, out_ref = refs[8:]
    live = lax.broadcasted_iota(jnp.int32, (1, TOK), 1) < mask_length(mask_ref)
    own = place_ref[2]
    for block in range(4):
        lanes = slice(block * 128, (block + 1) * 128)
        for head, source_ref in ((own, bias_ref), (1 - own, other_bias_ref)):
            for core in range(2):
                first, second = swap_halves(
                    source_ref[core, 2 * block].astype(F32), source_ref[core, 2 * block + 1].astype(F32)
                )
                full_bias_ref[head, :, core, 0, :, lanes] = first.astype(BF16)
                full_bias_ref[head, :, core, 1, :, lanes] = second.astype(BF16)
        halves = swap_halves(recv_ref[2 * block].astype(F32), recv_ref[2 * block + 1].astype(F32))
        for sample in range(2):
            half = halves[sample].astype(BF16)
            query_key_ref[sample, :, lanes] = half[: 2 * PAIR]
            for head in range(2):
                at = 2 * PAIR + head * HEAD
                value_ref[sample, head, :HEAD, lanes] = half[at : at + HEAD]
    value_ref[:, :, HEAD:, :] = jnp.ones((2, 2, 16, TOK), BF16)
    for head in range(2):
        bias = full_bias_ref[head].reshape(TOK, TOK)
        for sample in range(2):
            query = query_key_ref[sample, head * HEAD : (head + 1) * HEAD, :]
            key = query_key_ref[sample, PAIR + head * HEAD : PAIR + (head + 1) * HEAD, :]
            scores = dot(query, key, TN) * (HEAD**-0.5) + bias.astype(F32)
            scores = jnp.where(live, scores, -1e30)
            top = jnp.max(scores, axis=1, keepdims=True)
            weights = jnp.exp(scores - top).astype(BF16)
            mixed = dot(value_ref[sample, head], weights, NT)
            mixed_ref[sample, head * HEAD : (head + 1) * HEAD] = mixed[:HEAD] / mixed[HEAD : HEAD + 1]
    for block in range(4):
        lanes = slice(block * 128, (block + 1) * 128)
        first, second = swap_halves(mixed_ref[0, :, lanes], mixed_ref[1, :, lanes])
        out_ref[2 * block] = first.astype(BF16)
        out_ref[2 * block + 1] = second.astype(BF16)
    for slot in range(8):
        sends[slot][...] = out_ref[place_ref[3] ^ slot]


def tokens_out_kernel(place_ref, gate_ref, start_ref, weight_ref, *refs):
    out_ref, recv_ref = refs[8:]
    for slot in range(8):
        recv_ref[place_ref[3] ^ slot] = refs[slot][...]
    mixed = jnp.transpose(recv_ref[...].reshape(WIDTH, 128).astype(F32), (1, 0))
    blended = (gate_ref[...] * mixed).astype(BF16)
    out_ref[...] = (start_ref[...] + dot(blended, weight_ref[...])).reshape(2, 64, WIDTH)


def call(kernel, name, out_shape, scratch, *operands, smem=0, after=(), flops=10**8):
    shapes = jax.tree.leaves(out_shape)
    nbytes = sum(v.size * v.dtype.itemsize for v in (*operands, *shapes))
    vmem = pl.BlockSpec(memory_space=pltpu.VMEM)
    return pl.pallas_call(
        kernel,
        name=name,
        out_shape=out_shape,
        in_specs=[pl.BlockSpec(memory_space=pltpu.SMEM)] * smem
        + [vmem] * (len(operands) - smem)
        + [pl.BlockSpec(memory_space=pl.ANY)] * len(after),
        out_specs=jax.tree.map(lambda _: vmem, out_shape),
        scratch_shapes=scratch,
        cost_estimate=pl.CostEstimate(flops=flops, bytes_accessed=nbytes, transcendentals=0),
        compiler_params=pltpu.CompilerParams(vmem_limit_bytes=VMEM_LIMIT),
    )(*operands, *after)


def shape(*dims, dtype=F32):
    return jax.ShapeDtypeStruct(dims, dtype)


ALL = ("core", "col", "z")


def exchange(value, axes=ALL):
    return lax.all_to_all(value, axes, 0, 0, tiled=True)


def on_device(
    pair, pair_mask, prev_pair, diff_tokens, diff_mask, atom_feats, atom_token,
    trunk_in, trunk_out, bias_weight, atom_weight, attn_in, attn_out,
):
    z, core, col = lax.axis_index("z"), lax.axis_index("core"), lax.axis_index("col")
    place = jnp.stack([(z * 2 + core) * ROWS, col * COLS, core, col]).astype(jnp.int32)
    tile = (2, 16, COLS, C)
    send = shape(C, 32, 128, dtype=BF16)
    spread = pltpu.VMEM((C * 32, 128), F32)
    received = pltpu.VMEM((C * 16, 128), F32)
    square = pltpu.VMEM((8, 2, 2, 16, TOK), BF16)

    def product(gathered, outgoing, *bias, after):
        rows = 32 if bias else 16
        result = call(
            functools.partial(product_kernel, outgoing=outgoing), "product",
            shape(2, 8, 8, rows, 128, dtype=BF16), [square, square],
            gathered.reshape(2, 8, 8, 32, 128), *bias, after=after, flops=2 * TOK**3,
        )
        return exchange(result.reshape(C, rows, 128))

    def gate(values, update):
        return call(
            functools.partial(gate_kernel, update=update), "gate", shape(*tile), [], values, trunk_in
        )

    pair0 = pair.reshape(tile)
    operands = call(
        project_kernel, "project", send, [spread], place, pair_mask, pair0, trunk_in, smem=1
    )
    gathered = exchange(operands)

    bias_here = call(
        bias_kernel, "bias", shape(HEADS, 16, 128, dtype=BF16), [pltpu.VMEM((HEADS * 16, 128), F32)],
        prev_pair.reshape(tile), jnp.swapaxes(bias_weight, 0, 1), after=(operands,),
    )
    bias_other = lax.ppermute(bias_here, "grp", [(0, 1), (1, 0)])
    start, gate2, parts = call(
        tokens_kernel, "tokens_in",
        [shape(128, WIDTH), shape(128, WIDTH), shape(8, 3 * PAIR, 128, dtype=BF16)], [],
        place, diff_tokens[0], atom_feats[0], atom_token, atom_weight, attn_in, smem=1, after=(operands,),
    )

    summed0 = product(gathered, True, bias_other, after=(start,))
    gate0 = gate(pair0, 0)
    parts = exchange(parts, "col")

    pair1, operands = call(
        finish_project_kernel, "finish_project", (shape(*tile), send), [received, spread],
        place, pair_mask, summed0, pair0, gate0, trunk_out, trunk_in, smem=1,
    )
    gathered = exchange(operands)
    biases = summed0[:, 16:, :]
    other_biases = lax.ppermute(biases, "core", [(0, 1), (1, 0)])
    mixed = call(
        attention_kernel, "attention", [shape(PAIR, 128, dtype=BF16)] * 8,
        [
            pltpu.VMEM((2, 2 * PAIR, TOK), BF16),
            pltpu.VMEM((2, 2, HEAD + 16, TOK), BF16),
            pltpu.VMEM((2, 8, 2, 2, 16, TOK), BF16),
            pltpu.VMEM((2, PAIR, TOK), F32),
            pltpu.VMEM((8, PAIR, 128), BF16),
        ],
        place, diff_mask, parts, biases.reshape(2, 8, 8, 16, 128),
        other_biases.reshape(2, 8, 8, 16, 128), smem=1,
    )
    summed1 = product(gathered, False, after=(mixed[0],))
    mixed = [mixed[0]] + [
        lax.ppermute(mixed[slot], "col", [(at, at ^ slot) for at in range(8)]) for slot in range(1, 8)
    ]
    tokens_done = call(
        tokens_out_kernel, "tokens_out", shape(2, 64, WIDTH), [pltpu.VMEM((8, PAIR, 128), BF16)],
        place, gate2, start, attn_out, *mixed, smem=1,
    )
    gate1 = gate(pair1, 1)
    pair2 = call(
        finish_kernel, "finish", shape(*tile), [received],
        summed1, pair1, gate1, trunk_out, after=(tokens_done,),
    )
    return (pair2.reshape(1, ROWS, COLS, C), tokens_done[None])


def solution(mesh):
    split = Mesh(mesh.devices.reshape(2, 8, 2, 8), ("grp", "z", "core", "col"))
    row = ("z", "core")
    placed = (
        P("grp", row, "col", None),
        P("grp", None),
        P("grp", row, "col", None),
        P("grp", row, "col", None),
        P("grp", None),
        P("grp", row, "col", None),
        P("grp", "col"),
        P(),
        P(),
        P(),
        P(),
        P(),
        P(),
    )
    return jax.shard_map(
        on_device,
        mesh=split,
        in_specs=placed,
        out_specs=(P("grp", row, "col", None), P("grp", row, "col", None)),
        check_vma=False,
    )
```

```python
import functools

import jax
import jax.numpy as jnp
from jax import lax
from jax.experimental import pallas as pl
from jax.experimental.pallas import tpu as pltpu
from jax.sharding import Mesh, PartitionSpec as P

EPSILON = 1e-05
F32, BF16 = jnp.float32, jnp.bfloat16
ROWS, COLS, TOK, C = 32, 64, 512, 128
HEADS, HEAD = 16, 48
WIDTH, PAIR = HEADS * HEAD, 2 * HEAD
WIDE, MIDDLE, NARROW = 63_000_000, 40_000_000, 24 * 2**20
PITCH, RECV_PITCH = 40, 24
NT = (((1,), (1,)), ((), ()))
TN = (((0,), (0,)), ((), ()))


def dot(left, right, dims=(((1,), (0,)), ((), ()))):
    return lax.dot_general(left, right, dims, preferred_element_type=F32)


def layer_norm(values, axis=-1):
    centred = values - jnp.mean(values, axis=axis, keepdims=True)
    spread = jnp.mean(centred * centred, axis=axis, keepdims=True)
    return centred * lax.rsqrt(spread + EPSILON)


def low_lanes():
    return lax.broadcasted_iota(jnp.int32, (1, 128), 1) < 64


def swap_halves(first, second):
    low = low_lanes()
    axis = first.ndim - 1
    return (
        jnp.where(low, first, pltpu.roll(second, 64, axis)),
        jnp.where(low, pltpu.roll(first, 64, axis), second),
    )


def pair_step(pair_ref, step):
    return pair_ref[:, step].reshape(2 * COLS, C)


def turned(weight):
    return jnp.transpose(weight.astype(F32), (1, 0)).astype(BF16)


def project_step(values, step, length, row0, col0, weight, spread_ref):
    normed = layer_norm(values, 0).astype(BF16)
    lane = lax.broadcasted_iota(jnp.int32, (1, 128), 1)
    half = (lane >= 64).astype(jnp.int32)
    row = row0 + half * 16 + step
    col = col0 + lane - half * 64
    live = jnp.logical_and(row < length, col < length).astype(F32)
    projected = dot(weight, normed)
    left = live * jax.nn.sigmoid(projected[:C]) * projected[C : 2 * C]
    right = live * jax.nn.sigmoid(projected[2 * C : 3 * C]) * projected[3 * C :]
    spread_ref[pl.ds(step, C, stride=PITCH), :] = left
    spread_ref[pl.ds(step + 16, C, stride=PITCH), :] = right


def mask_length(mask_ref):
    return jnp.sum(mask_ref[...])


def send_out(spread_ref, stage_ref, out_ref, sems):
    copies = []
    for part in range(4):
        chunk = pl.ds(part * 32, 32)
        values = spread_ref[pl.ds(part * 32 * PITCH, 32 * PITCH), :].reshape(32, PITCH, 128)
        stage_ref[chunk] = values[:, :32].astype(BF16)
        copies.append(pltpu.make_async_copy(stage_ref.at[chunk], out_ref.at[chunk], sems.at[part]))
        copies[-1].start()
    for copy in copies:
        copy.wait()


def project_kernel(
    place_ref, mask_in, pair_in, weight_in, out_ref,
    mask_ref, pair_ref, weight_ref, spread_ref, stage_ref, in_sems, out_sems,
):
    copies = [
        pltpu.make_async_copy(mask_in, mask_ref, in_sems.at[4]),
        pltpu.make_async_copy(weight_in, weight_ref, in_sems.at[5]),
    ]
    for part in range(4):
        steps = pl.ds(part * 4, 4)
        copies.append(
            pltpu.make_async_copy(pair_in.at[:, steps], pair_ref.at[:, steps], in_sems.at[part])
        )
    for copy in copies:
        copy.start()
    copies[0].wait()
    copies[1].wait()
    length = mask_length(mask_ref)
    weight = turned(weight_ref[0, :, : 4 * C])
    for part in range(4):
        copies[2 + part].wait()
        for step in range(part * 4, part * 4 + 4):
            values = jnp.transpose(pair_step(pair_ref, step), (1, 0))
            project_step(values, step, length, place_ref[0], place_ref[1], weight, spread_ref)
    send_out(spread_ref, stage_ref, out_ref, out_sems)


def gate_kernel(pair_ref, weight_ref, *refs):
    pair_out_ref, gate_ref = refs[-2:]
    weight = turned(weight_ref[0, :, 4 * C :])
    for step in range(16):
        values = jnp.transpose(pair_step(pair_ref, step), (1, 0))
        pair_out_ref[step] = values
        gate_ref[step] = jax.nn.sigmoid(dot(weight, layer_norm(values, 0).astype(BF16)))


def gate_back_kernel(pair_ref, weight_ref, *refs):
    pair_out_ref, gate_ref = refs[-2:]
    weight = turned(weight_ref[1, :, 4 * C :])
    for step in range(16):
        values = pair_ref[step]
        gate = jax.nn.sigmoid(dot(weight, layer_norm(values, 0).astype(BF16)))
        pair_out_ref[:, step] = jnp.transpose(values, (1, 0)).reshape(2, COLS, C)
        gate_ref[:, step] = jnp.transpose(gate, (1, 0)).reshape(2, COLS, C)


def product_kernel(recv_ref, *refs, outgoing):
    out_ref, left_ref, right_ref = refs[-3:]
    if outgoing:
        bias_ref = refs[0]
        for core in range(2):
            for col in range(8):
                tile = bias_ref[2 * col + core]
                out_ref[core, col, :, 16:, :] = jnp.broadcast_to(tile[None], (8, 16, 128))
    for block in range(4):
        lanes = slice(block * 128, (block + 1) * 128)
        for side, dest_ref in ((0, left_ref), (1, right_ref)):
            rows = slice(side * 16, side * 16 + 16)
            for core in range(2):
                first, second = swap_halves(
                    recv_ref[core, 2 * block, :, rows, :].astype(F32),
                    recv_ref[core, 2 * block + 1, :, rows, :].astype(F32),
                )
                dest_ref[:, core, 0, :, lanes] = first.astype(BF16)
                dest_ref[:, core, 1, :, lanes] = second.astype(BF16)
    left = left_ref[...].reshape(TOK, TOK)
    right = right_ref[...].reshape(TOK, TOK)
    for block in range(4):
        lanes = slice(block * 128, (block + 1) * 128)
        if outgoing:
            summed = dot(left, right[lanes], NT)
        else:
            summed = dot(left, right[:, lanes], TN)
        summed = summed.reshape(8, 2, 2, 16, 128)
        for core in range(2):
            first, second = swap_halves(summed[:, core, 0], summed[:, core, 1])
            out_ref[core, 2 * block, :, :16, :] = first.astype(BF16)
            out_ref[core, 2 * block + 1, :, :16, :] = second.astype(BF16)


def load_summed(recv_ref, recv_f32_ref):
    recv_f32_ref.reshape(C, RECV_PITCH, 128)[:, :16] = recv_ref[:, :16, :].astype(F32)


def normed_sum(recv_f32_ref, step):
    return layer_norm(recv_f32_ref[pl.ds(step, C, stride=RECV_PITCH), :], 0).astype(BF16)


def finish_project_kernel(
    place_ref, mask_ref, recv_ref, pair_ref, gate_ref, out_weight_ref, in_weight_ref,
    pair_out_ref, out_ref, recv_f32_ref, spread_ref, stage_ref, out_sems,
):
    length = mask_length(mask_ref)
    weight = turned(in_weight_ref[1, :, : 4 * C])
    out_weight = turned(out_weight_ref[0])
    load_summed(recv_ref, recv_f32_ref)
    for step in range(16):
        update = dot(out_weight, normed_sum(recv_f32_ref, step))
        values = pair_ref[step] + gate_ref[step] * update
        pair_out_ref[step] = values
        project_step(values, step, length, place_ref[0], place_ref[1], weight, spread_ref)
    send_out(spread_ref, stage_ref, out_ref, out_sems)


def finish_kernel(recv_ref, pair_ref, gate_ref, out_weight_ref, out_ref, recv_f32_ref, stage_ref, sems):
    load_summed(recv_ref, recv_f32_ref)
    copies = []
    for part in range(4):
        for step in range(part * 4, part * 4 + 4):
            normed = normed_sum(recv_f32_ref, step).astype(F32)
            update = dot(jnp.transpose(normed, (1, 0)).astype(BF16), out_weight_ref[1])
            values = pair_step(pair_ref, step) + pair_step(gate_ref, step) * update
            stage_ref[:, step] = values.reshape(2, COLS, C)
        steps = pl.ds(part * 4, 4)
        copies.append(
            pltpu.make_async_copy(stage_ref.at[:, steps], out_ref.at[:, steps], sems.at[part])
        )
        copies[-1].start()
    for copy in copies:
        copy.wait()


def fence_kernel(*refs):
    refs[-1][...] = jnp.zeros_like(refs[-1])


def bias_kernel(prev_ref, weight_ref, *refs):
    out_ref, spread_ref = refs[-2:]

    def body(step, carry):
        normed = layer_norm(pair_step(prev_ref, step)).astype(BF16)
        spread_ref[pl.ds(step, HEADS, stride=16), :] = dot(weight_ref[...], normed, NT)
        return carry

    lax.fori_loop(0, 16, body, 0, unroll=4)
    out_ref[...] = spread_ref[...].astype(BF16).reshape(HEADS, 16, 128)


def copy_all(pairs, sems):
    copies = [
        pltpu.make_async_copy(source, dest, sems.at[index]) for index, (source, dest) in enumerate(pairs)
    ]
    for copy in copies:
        copy.start()
    return copies


def wait_all(copies):
    for copy in copies:
        copy.wait()


def tokens_kernel(
    place_ref, tokens_ref, atoms_ref, ids_ref, atom_weight_ref, weight_ref, *refs,
):
    start_out, gate_out, *sends = refs[-14:-4]
    start_ref, gate_ref, parts_ref, sems = refs[-4:]
    tokens, atoms = 64, 256
    local = ids_ref[...] - place_ref[1]
    onehot = (lax.broadcasted_iota(jnp.int32, (tokens, atoms), 0) == local).astype(F32)
    count = jnp.sum(onehot, axis=1, keepdims=True)
    onehot = onehot.astype(BF16)
    pooled = [(dot(onehot, atoms_ref[sample]) / count).astype(BF16) for sample in range(2)]
    start = tokens_ref[...].reshape(128, WIDTH) + dot(
        jnp.concatenate(pooled, axis=0), atom_weight_ref[...]
    )
    start_ref[...] = start
    normed = layer_norm(start).astype(BF16)
    for part in range(3):
        projected = dot(normed, weight_ref[:, part * WIDTH : (part + 1) * WIDTH])
        turned = jnp.transpose(projected, (1, 0)).astype(BF16)
        parts_ref[:, part * PAIR : (part + 1) * PAIR, :] = turned.reshape(8, PAIR, 128)
    copies = copy_all(
        [(parts_ref.at[place_ref[3] ^ slot], sends[slot]) for slot in range(8)] + [(start_ref, start_out)],
        sems,
    )
    gate_ref[...] = jax.nn.sigmoid(dot(normed, weight_ref[:, 3 * WIDTH :]))
    copies.append(pltpu.make_async_copy(gate_ref, gate_out, sems.at[9]))
    copies[-1].start()
    wait_all(copies)


def attention_kernel(place_ref, mask_ref, bias_ref, other_bias_ref, *refs):
    received, sends = refs[:8], refs[8:16]
    recv_ref, query_key_ref, value_ref, full_bias_ref, mixed_ref, out_ref, sems = refs[16:]
    own = place_ref[2]
    copies = copy_all(
        [(received[slot], recv_ref.at[place_ref[3] ^ slot]) for slot in range(8)], sems
    )
    live = lax.broadcasted_iota(jnp.int32, (1, TOK), 1) < mask_length(mask_ref)
    for block in range(4):
        lanes = slice(block * 128, (block + 1) * 128)
        for head, source_ref, rows in ((own, bias_ref, slice(16, 32)), (1 - own, other_bias_ref, slice(16))):
            for core in range(2):
                first, second = swap_halves(
                    source_ref[core, 2 * block, :, rows, :].astype(F32),
                    source_ref[core, 2 * block + 1, :, rows, :].astype(F32),
                )
                full_bias_ref[head, :, core, 0, :, lanes] = first.astype(BF16)
                full_bias_ref[head, :, core, 1, :, lanes] = second.astype(BF16)
    wait_all(copies)
    for block in range(4):
        lanes = slice(block * 128, (block + 1) * 128)
        halves = swap_halves(recv_ref[2 * block].astype(F32), recv_ref[2 * block + 1].astype(F32))
        for sample in range(2):
            half = halves[sample].astype(BF16)
            query_key_ref[sample, :, lanes] = half[: 2 * PAIR]
            for head in range(2):
                at = 2 * PAIR + head * HEAD
                value_ref[sample, head, :HEAD, lanes] = half[at : at + HEAD]
    value_ref[:, :, HEAD:, :] = jnp.ones((2, 2, 16, TOK), BF16)
    for head in range(2):
        bias = full_bias_ref[head].reshape(TOK, TOK)
        for sample in range(2):
            query = query_key_ref[sample, head * HEAD : (head + 1) * HEAD, :]
            key = query_key_ref[sample, PAIR + head * HEAD : PAIR + (head + 1) * HEAD, :]
            scores = dot(query, key, TN) * (HEAD**-0.5) + bias.astype(F32)
            scores = jnp.where(live, scores, -1e30)
            top = jnp.max(scores, axis=1, keepdims=True)
            weights = jnp.exp(scores - top).astype(BF16)
            mixed = dot(value_ref[sample, head], weights, NT)
            mixed_ref[sample, head * HEAD : (head + 1) * HEAD] = mixed[:HEAD] / mixed[HEAD : HEAD + 1]
    for block in range(4):
        lanes = slice(block * 128, (block + 1) * 128)
        first, second = swap_halves(mixed_ref[0, :, lanes], mixed_ref[1, :, lanes])
        out_ref[2 * block] = first.astype(BF16)
        out_ref[2 * block + 1] = second.astype(BF16)
    wait_all(copy_all([(out_ref.at[place_ref[3] ^ slot], sends[slot]) for slot in range(8)], sems))


def tokens_out_kernel(place_ref, gate_in, start_in, weight_in, *refs):
    received = refs[:8]
    out_ref, gate_ref, start_ref, weight_ref, recv_ref, sems = refs[8:]
    wait_all(
        copy_all(
            [(received[slot], recv_ref.at[place_ref[3] ^ slot]) for slot in range(8)]
            + [(gate_in, gate_ref), (start_in, start_ref), (weight_in, weight_ref)],
            sems,
        )
    )
    mixed = jnp.transpose(recv_ref[...].reshape(WIDTH, 128).astype(F32), (1, 0))
    blended = (gate_ref[...] * mixed).astype(BF16)
    out_ref[...] = (start_ref[...] + dot(blended, weight_ref[...])).reshape(2, 64, WIDTH)


def call(
    kernel, name, out_shape, scratch, *operands, smem=0, after=(), far=(), far_out=(), flops=10**8, limit=WIDE
):
    shapes = jax.tree.leaves(out_shape)
    nbytes = sum(v.size * v.dtype.itemsize for v in (*operands, *shapes))
    near = pl.BlockSpec(memory_space=pltpu.VMEM)
    anywhere = pl.BlockSpec(memory_space=pltpu.HBM)
    scalar = pl.BlockSpec(memory_space=pltpu.SMEM)
    outs = [anywhere if index in far_out else near for index in range(len(shapes))]
    return pl.pallas_call(
        kernel,
        name=name,
        out_shape=out_shape,
        in_specs=[
            scalar if index < smem else anywhere if index in far else near
            for index in range(len(operands))
        ]
        + [anywhere] * len(after),
        out_specs=outs if isinstance(out_shape, (list, tuple)) else outs[0],
        scratch_shapes=scratch,
        cost_estimate=pl.CostEstimate(flops=flops, bytes_accessed=nbytes, transcendentals=0),
        compiler_params=pltpu.CompilerParams(vmem_limit_bytes=limit),
    )(*operands, *after)


def shape(*dims, dtype=F32):
    return jax.ShapeDtypeStruct(dims, dtype)


ALL = ("core", "col", "z")


def exchange(value):
    return lax.all_to_all(value, ALL, 0, 0, tiled=True)


def swap(values, axis):
    return [values[0]] + [
        lax.ppermute(values[slot], axis, [(at, at ^ slot) for at in range(8)]) for slot in range(1, 8)
    ]


def on_device(
    pair, pair_mask, prev_pair, diff_tokens, diff_mask, atom_feats, atom_token,
    trunk_in, trunk_out, bias_weight, atom_weight, attn_in, attn_out,
):
    z, core, col = lax.axis_index("z"), lax.axis_index("core"), lax.axis_index("col")
    place = jnp.stack([(z * 2 + core) * ROWS, col * COLS, core, col, z]).astype(jnp.int32)
    tile = (2, 16, COLS, C)
    send = shape(C, 32, 128, dtype=BF16)
    spread = pltpu.VMEM((C * PITCH, 128), F32)
    stage = pltpu.VMEM((C, 32, 128), BF16)
    received = pltpu.VMEM((C * RECV_PITCH, 128), F32)
    square = pltpu.VMEM((8, 2, 2, 16, TOK), BF16)
    sems = pltpu.SemaphoreType.DMA((4,))

    def product(gathered, outgoing, extra):
        rows = 32 if outgoing else 16
        result = call(
            functools.partial(product_kernel, outgoing=outgoing), "product",
            shape(2, 8, 8, rows, 128, dtype=BF16), [square, square],
            gathered.reshape(2, 8, 8, 32, 128), extra, flops=2 * TOK**3, limit=NARROW,
        )
        return exchange(result.reshape(C, rows, 128))

    turned_tile = shape(16, C, 128)
    token_shape = shape(8, 128)

    pair0 = pair.reshape(tile)
    operands = call(
        project_kernel, "project", send,
        [
            pltpu.VMEM((1, TOK), jnp.int32), pltpu.VMEM(tile, F32), pltpu.VMEM((2, C, 5 * C), BF16),
            spread, stage, pltpu.SemaphoreType.DMA((6,)), sems,
        ],
        place, pair_mask, pair0, trunk_in, smem=1, far=(1, 2, 3), far_out=(0,),
    )
    gathered = exchange(operands)

    start, gate2, *parts = call(
        tokens_kernel, "tokens_in",
        [shape(128, WIDTH), shape(128, WIDTH)] + [shape(3 * PAIR, 128, dtype=BF16)] * 8,
        [
            pltpu.VMEM((128, WIDTH), F32), pltpu.VMEM((128, WIDTH), F32),
            pltpu.VMEM((8, 3 * PAIR, 128), BF16), pltpu.SemaphoreType.DMA((10,)),
        ],
        place, diff_tokens[0], atom_feats[0], atom_token, atom_weight, attn_in,
        smem=1, far_out=range(10), after=(operands,),
    )
    bias_here = call(
        bias_kernel, "bias", shape(HEADS, 16, 128, dtype=BF16), [pltpu.VMEM((HEADS * 16, 128), F32)],
        prev_pair.reshape(tile), jnp.swapaxes(bias_weight, 0, 1), after=(parts[0],),
    )
    bias_other = lax.ppermute(bias_here, "grp", [(0, 1), (1, 0)])

    summed0 = product(gathered, True, bias_other)
    parts = swap(parts, "col")
    pair0, gate0 = call(
        gate_kernel, "gate", [turned_tile, turned_tile], [], pair0, trunk_in, after=tuple(parts[1:]),
        limit=MIDDLE,
    )

    pair1, operands = call(
        finish_project_kernel, "finish_project", (turned_tile, send), [received, spread, stage, sems],
        place, pair_mask, summed0, pair0, gate0, trunk_out, trunk_in,
        smem=1, far_out=(1,), limit=NARROW,
    )
    gathered = exchange(operands)
    bias_far = lax.ppermute(summed0[:, 16:, :], "core", [(0, 1), (1, 0)])
    mixed = call(
        attention_kernel, "attention", [shape(PAIR, 128, dtype=BF16)] * 8,
        [
            pltpu.VMEM((8, 3 * PAIR, 128), BF16),
            pltpu.VMEM((2, 2 * PAIR, TOK), BF16),
            pltpu.VMEM((2, 2, HEAD + 16, TOK), BF16),
            pltpu.VMEM((2, 8, 2, 2, 16, TOK), BF16),
            pltpu.VMEM((2, PAIR, TOK), F32),
            pltpu.VMEM((8, PAIR, 128), BF16),
            pltpu.SemaphoreType.DMA((8,)),
        ],
        place, diff_mask, summed0.reshape(2, 8, 8, 32, 128), bias_far.reshape(2, 8, 8, 16, 128), *parts,
        smem=1, far=range(4, 12), far_out=range(8),
    )
    mixed = swap(mixed, "col")
    token = call(fence_kernel, "fence", token_shape, [], after=tuple(mixed[1:]))
    summed1 = product(gathered, False, token)
    tokens_done = call(
        tokens_out_kernel, "tokens_out", shape(2, 64, WIDTH),
        [
            pltpu.VMEM((128, WIDTH), F32), pltpu.VMEM((128, WIDTH), F32), pltpu.VMEM((WIDTH, WIDTH), BF16),
            pltpu.VMEM((8, PAIR, 128), BF16), pltpu.SemaphoreType.DMA((11,)),
        ],
        place, gate2, start, attn_out, *mixed, smem=1, far=range(1, 12),
    )
    pair1, gate1 = call(
        gate_back_kernel, "gate_back", [shape(*tile), shape(*tile)], [], pair1, trunk_in,
        after=(tokens_done,), limit=MIDDLE,
    )
    pair2 = call(
        finish_kernel, "finish", shape(*tile), [received, pltpu.VMEM(tile, F32), sems],
        summed1, pair1, gate1, trunk_out, far_out=(0,), limit=NARROW,
    )
    return (pair2.reshape(1, ROWS, COLS, C), tokens_done[None])


def solution(mesh):
    split = Mesh(mesh.devices.reshape(2, 8, 2, 8), ("grp", "z", "core", "col"))
    row = ("z", "core")
    placed = (
        P("grp", row, "col", None),
        P("grp", None),
        P("grp", row, "col", None),
        P("grp", row, "col", None),
        P("grp", None),
        P("grp", row, "col", None),
        P("grp", "col"),
        P(),
        P(),
        P(),
        P(),
        P(),
        P(),
    )
    return jax.shard_map(
        on_device,
        mesh=split,
        in_specs=placed,
        out_specs=(P("grp", row, "col", None), P("grp", row, "col", None)),
        check_vma=False,
    )
```

```python
import functools

import jax
import jax.numpy as jnp
from jax import lax
from jax.experimental import pallas as pl
from jax.experimental.pallas import tpu as pltpu
from jax.sharding import Mesh, PartitionSpec as P

EPSILON = 1e-05
F32, BF16 = jnp.float32, jnp.bfloat16
ROWS, COLS, TOK, C = 32, 64, 512, 128
HEADS, HEAD = 16, 48
WIDTH, PAIR = HEADS * HEAD, 2 * HEAD
WIDE, MIDDLE, NARROW = 63_000_000, 40_000_000, 24 * 2**20
FINISH = 24 * 2**20
PITCH, RECV_PITCH = 40, 24
NT = (((1,), (1,)), ((), ()))
TN = (((0,), (0,)), ((), ()))


def dot(left, right, dims=(((1,), (0,)), ((), ()))):
    return lax.dot_general(left, right, dims, preferred_element_type=F32)


def layer_norm(values, axis=-1):
    centred = values - jnp.mean(values, axis=axis, keepdims=True)
    spread = jnp.mean(centred * centred, axis=axis, keepdims=True)
    return centred * lax.rsqrt(spread + EPSILON)


def low_lanes():
    return lax.broadcasted_iota(jnp.int32, (1, 128), 1) < 64


def swap_halves(first, second):
    low = low_lanes()
    axis = first.ndim - 1
    return (
        jnp.where(low, first, pltpu.roll(second, 64, axis)),
        jnp.where(low, pltpu.roll(first, 64, axis), second),
    )


def pair_step(pair_ref, step):
    return pair_ref[:, step].reshape(2 * COLS, C)


def turned(weight):
    return jnp.transpose(weight.astype(F32), (1, 0)).astype(BF16)


def quarter_weight(weight):
    return turned(weight).reshape(4, 4, 32, C)


def project_out(normed_ref, weight, length, row0, col0, spread_ref, stage_ref, out_ref, sems):
    lane = lax.broadcasted_iota(jnp.int32, (1, 128), 1)
    half = (lane >= 64).astype(jnp.int32)
    col_live = col0 + lane - half * 64 < length
    copies = []
    for quarter in range(4):
        part_weight = jnp.concatenate([weight[part, quarter] for part in range(4)], axis=0)
        base = quarter * 32 * PITCH
        for step in range(16):
            live = jnp.logical_and(row0 + half * 16 + step < length, col_live).astype(F32)
            projected = dot(part_weight, normed_ref[step])
            left = live * jax.nn.sigmoid(projected[:32]) * projected[32:64]
            right = live * jax.nn.sigmoid(projected[64:96]) * projected[96:]
            spread_ref[pl.ds(base + step, 32, stride=PITCH), :] = left
            spread_ref[pl.ds(base + step + 16, 32, stride=PITCH), :] = right
        chunk = pl.ds(quarter * 32, 32)
        values = spread_ref[pl.ds(base, 32 * PITCH), :].reshape(32, PITCH, 128)
        stage_ref[chunk] = values[:, :32].astype(BF16)
        copies.append(pltpu.make_async_copy(stage_ref.at[chunk], out_ref.at[chunk], sems.at[quarter]))
        copies[-1].start()
    for copy in copies:
        copy.wait()


def mask_length(mask_ref):
    return jnp.sum(mask_ref[...])


def project_kernel(
    place_ref, mask_in, pair_in, weight_in, out_ref,
    mask_ref, pair_ref, weight_ref, normed_ref, spread_ref, stage_ref, in_sems, out_sems,
):
    copies = [
        pltpu.make_async_copy(mask_in, mask_ref, in_sems.at[4]),
        pltpu.make_async_copy(weight_in, weight_ref, in_sems.at[5]),
    ]
    for part in range(4):
        steps = pl.ds(part * 4, 4)
        copies.append(
            pltpu.make_async_copy(pair_in.at[:, steps], pair_ref.at[:, steps], in_sems.at[part])
        )
    for copy in copies:
        copy.start()
    copies[0].wait()
    copies[1].wait()
    length = mask_length(mask_ref)
    weight = quarter_weight(weight_ref[0, :, : 4 * C])
    for part in range(4):
        copies[2 + part].wait()
        for step in range(part * 4, part * 4 + 4):
            values = jnp.transpose(pair_step(pair_ref, step), (1, 0))
            normed_ref[step] = layer_norm(values, 0).astype(BF16)
    project_out(
        normed_ref, weight, length, place_ref[0], place_ref[1], spread_ref, stage_ref, out_ref, out_sems
    )


def turn_kernel(pair_ref, *refs):
    for step in range(16):
        refs[-1][step] = jnp.transpose(pair_step(pair_ref, step), (1, 0))


def gate_back_kernel(pair_ref, weight_ref, *refs):
    pair_out_ref, gate_ref = refs[-2:]
    weight = turned(weight_ref[1, :, 4 * C :])
    for step in range(16):
        values = pair_ref[step]
        gate = jax.nn.sigmoid(dot(weight, layer_norm(values, 0).astype(BF16)))
        pair_out_ref[:, step] = jnp.transpose(values, (1, 0)).reshape(2, COLS, C)
        gate_ref[:, step] = jnp.transpose(gate, (1, 0)).reshape(2, COLS, C)


def tiles_to_rows(recv_ref, rows, channel, dest):
    for block in range(4):
        lanes = slice(block * 128, (block + 1) * 128)
        halves = swap_halves(
            recv_ref[:, 2 * block, channel, rows, :].astype(F32),
            recv_ref[:, 2 * block + 1, channel, rows, :].astype(F32),
        )
        for half in range(2):
            ref, index = dest(half, lanes)
            ref[index] = halves[half].astype(BF16)


def outgoing_kernel(place_ref, recv_ref, far_ref, bias_ref, out_ref, left_ref, right_ref):
    own = place_ref[2]
    for head in range(2):
        for col in range(8):
            tile = bias_ref[2 * col + head]
            rows = slice(32 + 16 * head, 48 + 16 * head)
            out_ref[:, col, rows, :] = jnp.broadcast_to(tile[None], (8, 16, 128))
    for channel in range(2):
        tiles_to_rows(
            recv_ref, slice(16), channel,
            lambda half, lanes: (left_ref, (channel, slice(None), half, slice(None), lanes)),
        )
        for core, ref, rows in ((own, recv_ref, slice(16, 32)), (1 - own, far_ref, slice(16))):
            tiles_to_rows(
                ref, rows, channel,
                lambda half, lanes: (right_ref, (channel, slice(None), core, half, slice(None), lanes)),
            )
        left = left_ref[channel].reshape(TOK // 2, TOK)
        right = right_ref[channel].reshape(TOK, TOK)
        rows = slice(16 * channel, 16 * channel + 16)
        for block in range(4):
            summed = dot(left, right[block * 128 : (block + 1) * 128], NT).reshape(8, 2, 16, 128)
            first, second = swap_halves(summed[:, 0], summed[:, 1])
            out_ref[:, 2 * block, rows, :] = first.astype(BF16)
            out_ref[:, 2 * block + 1, rows, :] = second.astype(BF16)


def take_right_kernel(recv_ref, bias_ref, out_ref):
    out_ref[...] = recv_ref[:, :, :, 16:, :]


def incoming_kernel(place_ref, recv_ref, token_ref, own_ref, far_ref, left_ref, right_ref):
    first_core = place_ref[2] == 0
    for channel in range(2):
        for ref, rows in ((left_ref, slice(16)), (right_ref, slice(16, 32))):
            tiles_to_rows(
                recv_ref, rows, channel,
                lambda half, lanes: (ref, (channel, slice(None), half, slice(None), lanes)),
            )
        left = left_ref[channel].reshape(TOK // 2, TOK)
        right = right_ref[channel].reshape(TOK // 2, TOK)
        rows = slice(16 * channel, 16 * channel + 16)
        for block in range(4):
            summed = dot(left, right[:, block * 128 : (block + 1) * 128], TN).reshape(8, 2, 2, 16, 128)
            for out_ref, kept in (
                (own_ref, jnp.where(first_core, summed[:, 0], summed[:, 1])),
                (far_ref, jnp.where(first_core, summed[:, 1], summed[:, 0])),
            ):
                first, second = swap_halves(kept[:, 0], kept[:, 1])
                out_ref[:, 2 * block, rows, :] = first.astype(BF16)
                out_ref[:, 2 * block + 1, rows, :] = second.astype(BF16)


def add_kernel(own_ref, far_ref, out_ref):
    out_ref[...] = (own_ref[...].astype(F32) + far_ref[...].astype(F32)).astype(BF16)


def load_summed(recv_ref, recv_f32_ref):
    recv_f32_ref.reshape(C, RECV_PITCH, 128)[:, :16] = recv_ref[:, :32, :].reshape(C, 16, 128).astype(F32)


def normed_sum(recv_f32_ref, step):
    return layer_norm(recv_f32_ref[pl.ds(step, C, stride=RECV_PITCH), :], 0).astype(BF16)


def finish_project_kernel(
    place_ref, mask_ref, recv_ref, pair_ref, out_weight_ref, in_weight_ref,
    pair_out_ref, out_ref, recv_f32_ref, normed_ref, spread_ref, stage_ref, out_sems,
):
    length = mask_length(mask_ref)
    weight = quarter_weight(in_weight_ref[1, :, : 4 * C])
    gate_weight = turned(in_weight_ref[0, :, 4 * C :])
    out_weight = turned(out_weight_ref[0])
    load_summed(recv_ref, recv_f32_ref)
    for step in range(16):
        values = pair_ref[step]
        gate = jax.nn.sigmoid(dot(gate_weight, layer_norm(values, 0).astype(BF16)))
        values = values + gate * dot(out_weight, normed_sum(recv_f32_ref, step))
        pair_out_ref[step] = values
        normed_ref[step] = layer_norm(values, 0).astype(BF16)
    project_out(
        normed_ref, weight, length, place_ref[0], place_ref[1], spread_ref, stage_ref, out_ref, out_sems
    )


def finish_kernel(recv_ref, pair_ref, gate_ref, out_weight_ref, out_ref, recv_f32_ref, stage_ref, sems):
    load_summed(recv_ref, recv_f32_ref)
    copies = []
    for part in range(4):
        for step in range(part * 4, part * 4 + 4):
            normed = normed_sum(recv_f32_ref, step).astype(F32)
            update = dot(jnp.transpose(normed, (1, 0)).astype(BF16), out_weight_ref[1])
            values = pair_step(pair_ref, step) + pair_step(gate_ref, step) * update
            stage_ref[:, step] = values.reshape(2, COLS, C)
        steps = pl.ds(part * 4, 4)
        copies.append(
            pltpu.make_async_copy(stage_ref.at[:, steps], out_ref.at[:, steps], sems.at[part])
        )
        copies[-1].start()
    for copy in copies:
        copy.wait()


def fence_kernel(*refs):
    refs[-1][...] = jnp.zeros_like(refs[-1])


def bias_kernel(prev_ref, weight_ref, *refs):
    out_ref, spread_ref = refs[-2:]

    def body(step, carry):
        normed = layer_norm(pair_step(prev_ref, step)).astype(BF16)
        spread_ref[pl.ds(step, HEADS, stride=16), :] = dot(weight_ref[...], normed, NT)
        return carry

    lax.fori_loop(0, 16, body, 0, unroll=4)
    out_ref[...] = spread_ref[...].astype(BF16).reshape(HEADS, 16, 128)


def copy_all(pairs, sems):
    copies = [
        pltpu.make_async_copy(source, dest, sems.at[index]) for index, (source, dest) in enumerate(pairs)
    ]
    for copy in copies:
        copy.start()
    return copies


def wait_all(copies):
    for copy in copies:
        copy.wait()


def tokens_kernel(
    place_ref, tokens_ref, atoms_ref, ids_ref, atom_weight_ref, weight_ref, *refs,
):
    start_out, gate_out, *sends = refs[-14:-4]
    start_ref, gate_ref, parts_ref, sems = refs[-4:]
    tokens, atoms = 64, 256
    local = ids_ref[...] - place_ref[1]
    onehot = (lax.broadcasted_iota(jnp.int32, (tokens, atoms), 0) == local).astype(F32)
    count = jnp.sum(onehot, axis=1, keepdims=True)
    onehot = onehot.astype(BF16)
    pooled = [(dot(onehot, atoms_ref[sample]) / count).astype(BF16) for sample in range(2)]
    start = tokens_ref[...].reshape(128, WIDTH) + dot(
        jnp.concatenate(pooled, axis=0), atom_weight_ref[...]
    )
    start_ref[...] = start
    normed = layer_norm(start).astype(BF16)
    for part in range(3):
        projected = dot(normed, weight_ref[:, part * WIDTH : (part + 1) * WIDTH])
        turned = jnp.transpose(projected, (1, 0)).astype(BF16)
        parts_ref[:, part * PAIR : (part + 1) * PAIR, :] = turned.reshape(8, PAIR, 128)
    copies = copy_all(
        [(parts_ref.at[place_ref[3] ^ slot], sends[slot]) for slot in range(8)] + [(start_ref, start_out)],
        sems,
    )
    gate_ref[...] = jax.nn.sigmoid(dot(normed, weight_ref[:, 3 * WIDTH :]))
    copies.append(pltpu.make_async_copy(gate_ref, gate_out, sems.at[9]))
    copies[-1].start()
    wait_all(copies)


def attention_kernel(place_ref, mask_ref, bias_ref, other_bias_ref, *refs):
    received, sends = refs[:8], refs[8:16]
    recv_ref, query_key_ref, value_ref, full_bias_ref, mixed_ref, out_ref, sems = refs[16:]
    own = place_ref[2]
    copies = copy_all(
        [(received[slot], recv_ref.at[place_ref[3] ^ slot]) for slot in range(8)], sems
    )
    live = lax.broadcasted_iota(jnp.int32, (1, TOK), 1) < mask_length(mask_ref)
    for block in range(4):
        lanes = slice(block * 128, (block + 1) * 128)
        for core, source_ref, base in ((own, bias_ref, 32), (1 - own, other_bias_ref, 0)):
            for head in range(2):
                rows = slice(base + 16 * head, base + 16 * head + 16)
                first, second = swap_halves(
                    source_ref[:, 2 * block, rows, :].astype(F32),
                    source_ref[:, 2 * block + 1, rows, :].astype(F32),
                )
                full_bias_ref[head, :, core, 0, :, lanes] = first.astype(BF16)
                full_bias_ref[head, :, core, 1, :, lanes] = second.astype(BF16)
    wait_all(copies)
    for block in range(4):
        lanes = slice(block * 128, (block + 1) * 128)
        halves = swap_halves(recv_ref[2 * block].astype(F32), recv_ref[2 * block + 1].astype(F32))
        for sample in range(2):
            half = halves[sample].astype(BF16)
            query_key_ref[sample, :, lanes] = half[: 2 * PAIR]
            for head in range(2):
                at = 2 * PAIR + head * HEAD
                value_ref[sample, head, :HEAD, lanes] = half[at : at + HEAD]
    value_ref[:, :, HEAD:, :] = jnp.ones((2, 2, 16, TOK), BF16)
    for head in range(2):
        bias = full_bias_ref[head].reshape(TOK, TOK)
        for sample in range(2):
            query = query_key_ref[sample, head * HEAD : (head + 1) * HEAD, :]
            key = query_key_ref[sample, PAIR + head * HEAD : PAIR + (head + 1) * HEAD, :]
            scores = dot(query, key, TN) * (HEAD**-0.5) + bias.astype(F32)
            scores = jnp.where(live, scores, -1e30)
            top = jnp.max(scores, axis=1, keepdims=True)
            weights = jnp.exp(scores - top).astype(BF16)
            mixed = dot(value_ref[sample, head], weights, NT)
            mixed_ref[sample, head * HEAD : (head + 1) * HEAD] = mixed[:HEAD] / mixed[HEAD : HEAD + 1]
    for block in range(4):
        lanes = slice(block * 128, (block + 1) * 128)
        first, second = swap_halves(mixed_ref[0, :, lanes], mixed_ref[1, :, lanes])
        out_ref[2 * block] = first.astype(BF16)
        out_ref[2 * block + 1] = second.astype(BF16)
    wait_all(copy_all([(out_ref.at[place_ref[3] ^ slot], sends[slot]) for slot in range(8)], sems))


def tokens_out_kernel(place_ref, gate_in, start_in, weight_in, *refs):
    received = refs[:8]
    out_ref, gate_ref, start_ref, weight_ref, recv_ref, sems = refs[8:]
    wait_all(
        copy_all(
            [(received[slot], recv_ref.at[place_ref[3] ^ slot]) for slot in range(8)]
            + [(gate_in, gate_ref), (start_in, start_ref), (weight_in, weight_ref)],
            sems,
        )
    )
    mixed = jnp.transpose(recv_ref[...].reshape(WIDTH, 128).astype(F32), (1, 0))
    blended = (gate_ref[...] * mixed).astype(BF16)
    out_ref[...] = (start_ref[...] + dot(blended, weight_ref[...])).reshape(2, 64, WIDTH)


def call(
    kernel, name, out_shape, scratch, *operands, smem=0, after=(), far=(), far_out=(), flops=10**8, limit=WIDE
):
    shapes = jax.tree.leaves(out_shape)
    nbytes = sum(v.size * v.dtype.itemsize for v in (*operands, *shapes))
    near = pl.BlockSpec(memory_space=pltpu.VMEM)
    anywhere = pl.BlockSpec(memory_space=pltpu.HBM)
    scalar = pl.BlockSpec(memory_space=pltpu.SMEM)
    outs = [anywhere if index in far_out else near for index in range(len(shapes))]
    return pl.pallas_call(
        kernel,
        name=name,
        out_shape=out_shape,
        in_specs=[
            scalar if index < smem else anywhere if index in far else near
            for index in range(len(operands))
        ]
        + [anywhere] * len(after),
        out_specs=outs if isinstance(out_shape, (list, tuple)) else outs[0],
        scratch_shapes=scratch,
        cost_estimate=pl.CostEstimate(flops=flops, bytes_accessed=nbytes, transcendentals=0),
        compiler_params=pltpu.CompilerParams(vmem_limit_bytes=limit),
    )(*operands, *after)


def shape(*dims, dtype=F32):
    return jax.ShapeDtypeStruct(dims, dtype)


ALL = ("z", "col")
EARLY, LATE = 4, 6


def from_other_core(value):
    return lax.ppermute(value, "core", [(0, 1), (1, 0)])


def exchange(value):
    return lax.all_to_all(value, ALL, 0, 0, tiled=True)


def swap(values, axis):
    return [values[0]] + [
        lax.ppermute(values[slot], axis, [(at, at ^ slot) for at in range(8)]) for slot in range(1, 8)
    ]


def on_device(
    pair, pair_mask, prev_pair, diff_tokens, diff_mask, atom_feats, atom_token,
    trunk_in, trunk_out, bias_weight, atom_weight, attn_in, attn_out,
):
    z, core, col = lax.axis_index("z"), lax.axis_index("core"), lax.axis_index("col")
    place = jnp.stack([(z * 2 + core) * ROWS, col * COLS, core, col, z]).astype(jnp.int32)
    tile = (2, 16, COLS, C)
    send = shape(C, 32, 128, dtype=BF16)
    normed = pltpu.VMEM((16, C, 128), BF16)
    spread = pltpu.VMEM((C * PITCH, 128), F32)
    stage = pltpu.VMEM((C, 32, 128), BF16)
    received = pltpu.VMEM((C * RECV_PITCH, 128), F32)
    half = pltpu.VMEM((2, 8, 2, 16, TOK), BF16)
    sums = shape(8, 8, 32, 128, dtype=BF16)
    sems = pltpu.SemaphoreType.DMA((4,))

    turned_tile = shape(16, C, 128)
    token_shape = shape(8, 128)

    pair0 = pair.reshape(tile)
    operands = call(
        project_kernel, "project", send,
        [
            pltpu.VMEM((1, TOK), jnp.int32), pltpu.VMEM(tile, F32), pltpu.VMEM((2, C, 5 * C), BF16),
            normed, spread, stage, pltpu.SemaphoreType.DMA((6,)), sems,
        ],
        place, pair_mask, pair0, trunk_in, smem=1, far=(1, 2, 3), far_out=(0,),
    )
    gathered = exchange(operands.reshape(64, 64, 128)).reshape(8, 8, 2, 32, 128)

    start, gate2, *parts = call(
        tokens_kernel, "tokens_in",
        [shape(128, WIDTH), shape(128, WIDTH)] + [shape(3 * PAIR, 128, dtype=BF16)] * 8,
        [
            pltpu.VMEM((128, WIDTH), F32), pltpu.VMEM((128, WIDTH), F32),
            pltpu.VMEM((8, 3 * PAIR, 128), BF16), pltpu.SemaphoreType.DMA((10,)),
        ],
        place, diff_tokens[0], atom_feats[0], atom_token, atom_weight, attn_in,
        smem=1, far_out=range(10), after=(operands,),
    )
    parts = swap(parts, "col")
    bias_here = call(
        bias_kernel, "bias", shape(HEADS, 16, 128, dtype=BF16), [pltpu.VMEM((HEADS * 16, 128), F32)],
        prev_pair.reshape(tile), jnp.swapaxes(bias_weight, 0, 1), after=tuple(parts[1:EARLY]),
    )
    bias_other = lax.ppermute(bias_here, "grp", [(0, 1), (1, 0)])

    right = call(
        take_right_kernel, "take_right", shape(8, 8, 2, 16, 128, dtype=BF16), [],
        gathered, bias_other, limit=NARROW,
    )
    summed0 = call(
        outgoing_kernel, "outgoing", shape(8, 8, 64, 128, dtype=BF16),
        [half, pltpu.VMEM((2, 8, 2, 2, 16, TOK), BF16)],
        place, gathered, from_other_core(right), bias_other,
        smem=1, flops=2 * TOK**3, limit=NARROW,
    )
    summed0 = exchange(summed0.reshape(64, 64, 128))
    token = call(fence_kernel, "fence", token_shape, [], after=tuple(parts[EARLY:]))
    pair0 = call(turn_kernel, "turn", turned_tile, [], pair0, after=(token,), limit=NARROW)

    pair1, operands = call(
        finish_project_kernel, "finish_project", (turned_tile, send), [received, normed, spread, stage, sems],
        place, pair_mask, summed0, pair0, trunk_out, trunk_in,
        smem=1, far_out=(1,), limit=FINISH,
    )
    gathered = exchange(operands.reshape(64, 64, 128)).reshape(8, 8, 2, 32, 128)
    bias_far = from_other_core(summed0[:, 32:, :])
    mixed = call(
        attention_kernel, "attention", [shape(PAIR, 128, dtype=BF16)] * 8,
        [
            pltpu.VMEM((8, 3 * PAIR, 128), BF16),
            pltpu.VMEM((2, 2 * PAIR, TOK), BF16),
            pltpu.VMEM((2, 2, HEAD + 16, TOK), BF16),
            pltpu.VMEM((2, 8, 2, 2, 16, TOK), BF16),
            pltpu.VMEM((2, PAIR, TOK), F32),
            pltpu.VMEM((8, PAIR, 128), BF16),
            pltpu.SemaphoreType.DMA((8,)),
        ],
        place, diff_mask, summed0.reshape(8, 8, 64, 128), bias_far.reshape(8, 8, 32, 128), *parts,
        smem=1, far=range(4, 12), far_out=range(8),
    )
    mixed = swap(mixed, "col")
    token = call(fence_kernel, "fence", token_shape, [], after=tuple(mixed[1:LATE]))
    own, far = call(
        incoming_kernel, "incoming", [sums, sums], [half, half],
        place, gathered, token, smem=1, flops=2 * TOK**3, limit=NARROW,
    )
    summed1 = call(add_kernel, "add", sums, [], own, from_other_core(far), limit=NARROW)
    summed1 = exchange(summed1.reshape(64, 32, 128))
    tokens_done = call(
        tokens_out_kernel, "tokens_out", shape(2, 64, WIDTH),
        [
            pltpu.VMEM((128, WIDTH), F32), pltpu.VMEM((128, WIDTH), F32), pltpu.VMEM((WIDTH, WIDTH), BF16),
            pltpu.VMEM((8, PAIR, 128), BF16), pltpu.SemaphoreType.DMA((11,)),
        ],
        place, gate2, start, attn_out, *mixed, smem=1, far=range(1, 12),
    )
    pair1, gate1 = call(
        gate_back_kernel, "gate_back", [shape(*tile), shape(*tile)], [], pair1, trunk_in,
        after=(tokens_done,), limit=MIDDLE,
    )
    pair2 = call(
        finish_kernel, "finish", shape(*tile), [received, pltpu.VMEM(tile, F32), sems],
        summed1, pair1, gate1, trunk_out, far_out=(0,), limit=NARROW,
    )
    return (pair2.reshape(1, ROWS, COLS, C), tokens_done[None])


def solution(mesh):
    split = Mesh(mesh.devices.reshape(2, 8, 2, 8), ("grp", "z", "core", "col"))
    row = ("z", "core")
    placed = (
        P("grp", row, "col", None),
        P("grp", None),
        P("grp", row, "col", None),
        P("grp", row, "col", None),
        P("grp", None),
        P("grp", row, "col", None),
        P("grp", "col"),
        P(),
        P(),
        P(),
        P(),
        P(),
        P(),
    )
    return jax.shard_map(
        on_device,
        mesh=split,
        in_specs=placed,
        out_specs=(P("grp", row, "col", None), P("grp", row, "col", None)),
        check_vma=False,
    )
```

```python
import functools

import jax
import jax.numpy as jnp
from jax import lax
from jax.experimental import pallas as pl
from jax.experimental.pallas import tpu as pltpu
from jax.sharding import Mesh, PartitionSpec as P

EPSILON = 1e-05
F32, BF16 = jnp.float32, jnp.bfloat16
ROWS, COLS, TOK, C = 32, 64, 512, 128
HEADS, HEAD = 16, 48
WIDTH, PAIR = HEADS * HEAD, 2 * HEAD
WIDE, MIDDLE, NARROW = 63_000_000, 40_000_000, 24 * 2**20
FINISH = 24 * 2**20
PITCH, RECV_PITCH = 40, 24
NT = (((1,), (1,)), ((), ()))
TN = (((0,), (0,)), ((), ()))


def dot(left, right, dims=(((1,), (0,)), ((), ()))):
    return lax.dot_general(left, right, dims, preferred_element_type=F32)


def layer_norm(values, axis=-1):
    centred = values - jnp.mean(values, axis=axis, keepdims=True)
    spread = jnp.mean(centred * centred, axis=axis, keepdims=True)
    return centred * lax.rsqrt(spread + EPSILON)


def low_lanes():
    return lax.broadcasted_iota(jnp.int32, (1, 128), 1) < 64


def swap_halves(first, second):
    low = low_lanes()
    axis = first.ndim - 1
    return (
        jnp.where(low, first, pltpu.roll(second, 64, axis)),
        jnp.where(low, pltpu.roll(first, 64, axis), second),
    )


def pair_step(pair_ref, step):
    return pair_ref[:, step].reshape(2 * COLS, C)


def turned(weight):
    return jnp.transpose(weight.astype(F32), (1, 0)).astype(BF16)


def quarter_weight(weight):
    return turned(weight).reshape(4, 4, 32, C)


def project_out(normed_ref, weight, length, row0, col0, spread_ref, stage_ref, out_ref, sems):
    lane = lax.broadcasted_iota(jnp.int32, (1, 128), 1)
    half = (lane >= 64).astype(jnp.int32)
    col_live = col0 + lane - half * 64 < length
    copies = []
    for quarter in range(4):
        part_weight = jnp.concatenate([weight[part, quarter] for part in range(4)], axis=0)
        base = quarter * 32 * PITCH
        for step in range(16):
            live = jnp.logical_and(row0 + half * 16 + step < length, col_live).astype(F32)
            projected = dot(part_weight, normed_ref[step])
            left = live * jax.nn.sigmoid(projected[:32]) * projected[32:64]
            right = live * jax.nn.sigmoid(projected[64:96]) * projected[96:]
            spread_ref[pl.ds(base + step, 32, stride=PITCH), :] = left
            spread_ref[pl.ds(base + step + 16, 32, stride=PITCH), :] = right
        chunk = pl.ds(quarter * 32, 32)
        values = spread_ref[pl.ds(base, 32 * PITCH), :].reshape(32, PITCH, 128)
        stage_ref[chunk] = values[:, :32].astype(BF16)
        copies.append(pltpu.make_async_copy(stage_ref.at[chunk], out_ref.at[chunk], sems.at[quarter]))
        copies[-1].start()
    for copy in copies:
        copy.wait()


def mask_length(mask_ref):
    return jnp.sum(mask_ref[...])


def project_kernel(
    place_ref, mask_in, pair_in, weight_in, out_ref,
    mask_ref, pair_ref, weight_ref, normed_ref, spread_ref, stage_ref, in_sems, out_sems,
):
    copies = [
        pltpu.make_async_copy(mask_in, mask_ref, in_sems.at[4]),
        pltpu.make_async_copy(weight_in, weight_ref, in_sems.at[5]),
    ]
    for part in range(4):
        steps = pl.ds(part * 4, 4)
        copies.append(
            pltpu.make_async_copy(pair_in.at[:, steps], pair_ref.at[:, steps], in_sems.at[part])
        )
    for copy in copies:
        copy.start()
    copies[0].wait()
    copies[1].wait()
    length = mask_length(mask_ref)
    weight = quarter_weight(weight_ref[0, :, : 4 * C])
    for part in range(4):
        copies[2 + part].wait()
        for step in range(part * 4, part * 4 + 4):
            values = jnp.transpose(pair_step(pair_ref, step), (1, 0))
            normed_ref[step] = layer_norm(values, 0).astype(BF16)
    project_out(
        normed_ref, weight, length, place_ref[0], place_ref[1], spread_ref, stage_ref, out_ref, out_sems
    )


def turn_kernel(pair_ref, *refs):
    for step in range(16):
        refs[-1][step] = jnp.transpose(pair_step(pair_ref, step), (1, 0))


def gate_back_kernel(pair_ref, weight_ref, *refs):
    pair_out_ref, gate_ref = refs[-2:]
    weight = turned(weight_ref[1, :, 4 * C :])
    for step in range(16):
        values = pair_ref[step]
        gate = jax.nn.sigmoid(dot(weight, layer_norm(values, 0).astype(BF16)))
        pair_out_ref[:, step] = jnp.transpose(values, (1, 0)).reshape(2, COLS, C)
        gate_ref[:, step] = jnp.transpose(gate, (1, 0)).reshape(2, COLS, C)


def tiles_to_rows(recv_ref, rows, channel, dest):
    for block in range(4):
        lanes = slice(block * 128, (block + 1) * 128)
        halves = swap_halves(
            recv_ref[:, 2 * block, channel, rows, :].astype(F32),
            recv_ref[:, 2 * block + 1, channel, rows, :].astype(F32),
        )
        for half in range(2):
            ref, index = dest(half, lanes)
            ref[index] = halves[half].astype(BF16)


def outgoing_kernel(place_ref, recv_ref, far_ref, bias_ref, out_ref, left_ref, right_ref):
    own = place_ref[2]
    for head in range(2):
        for col in range(8):
            tile = bias_ref[2 * col + head]
            rows = slice(32 + 16 * head, 48 + 16 * head)
            out_ref[:, col, rows, :] = jnp.broadcast_to(tile[None], (8, 16, 128))
    for channel in range(2):
        tiles_to_rows(
            recv_ref, slice(16), channel,
            lambda half, lanes: (left_ref, (channel, slice(None), half, slice(None), lanes)),
        )
        for core, ref, rows in ((own, recv_ref, slice(16, 32)), (1 - own, far_ref, slice(16))):
            tiles_to_rows(
                ref, rows, channel,
                lambda half, lanes: (right_ref, (channel, slice(None), core, half, slice(None), lanes)),
            )
        left = left_ref[channel].reshape(TOK // 2, TOK)
        right = right_ref[channel].reshape(TOK, TOK)
        rows = slice(16 * channel, 16 * channel + 16)
        for block in range(4):
            summed = dot(left, right[block * 128 : (block + 1) * 128], NT).reshape(8, 2, 16, 128)
            first, second = swap_halves(summed[:, 0], summed[:, 1])
            out_ref[:, 2 * block, rows, :] = first.astype(BF16)
            out_ref[:, 2 * block + 1, rows, :] = second.astype(BF16)


def take_right_kernel(recv_ref, bias_ref, out_ref):
    out_ref[...] = recv_ref[:, :, :, 16:, :]


def incoming_kernel(place_ref, recv_ref, token_ref, own_ref, far_ref, left_ref, right_ref):
    first_core = place_ref[2] == 0
    for channel in range(2):
        for ref, rows in ((left_ref, slice(16)), (right_ref, slice(16, 32))):
            tiles_to_rows(
                recv_ref, rows, channel,
                lambda half, lanes: (ref, (channel, slice(None), half, slice(None), lanes)),
            )
        left = left_ref[channel].reshape(TOK // 2, TOK)
        right = right_ref[channel].reshape(TOK // 2, TOK)
        rows = slice(16 * channel, 16 * channel + 16)
        for block in range(4):
            summed = dot(left, right[:, block * 128 : (block + 1) * 128], TN).reshape(8, 2, 2, 16, 128)
            for out_ref, kept in (
                (own_ref, jnp.where(first_core, summed[:, 0], summed[:, 1])),
                (far_ref, jnp.where(first_core, summed[:, 1], summed[:, 0])),
            ):
                first, second = swap_halves(kept[:, 0], kept[:, 1])
                out_ref[:, 2 * block, rows, :] = first.astype(BF16)
                out_ref[:, 2 * block + 1, rows, :] = second.astype(BF16)


def add_kernel(own_ref, far_ref, out_ref):
    out_ref[...] = (own_ref[...].astype(F32) + far_ref[...].astype(F32)).astype(BF16)


def load_summed(recv_ref, recv_f32_ref):
    recv_f32_ref.reshape(C, RECV_PITCH, 128)[:, :16] = recv_ref[:, :32, :].reshape(C, 16, 128).astype(F32)


def normed_sum(recv_f32_ref, step):
    return layer_norm(recv_f32_ref[pl.ds(step, C, stride=RECV_PITCH), :], 0).astype(BF16)


def finish_project_kernel(
    place_ref, mask_ref, recv_ref, pair_ref, out_weight_ref, in_weight_ref,
    pair_out_ref, out_ref, recv_f32_ref, normed_ref, spread_ref, stage_ref, out_sems,
):
    length = mask_length(mask_ref)
    weight = quarter_weight(in_weight_ref[1, :, : 4 * C])
    gate_weight = turned(in_weight_ref[0, :, 4 * C :])
    out_weight = turned(out_weight_ref[0])
    load_summed(recv_ref, recv_f32_ref)
    for step in range(16):
        values = pair_ref[step]
        gate = jax.nn.sigmoid(dot(gate_weight, layer_norm(values, 0).astype(BF16)))
        values = values + gate * dot(out_weight, normed_sum(recv_f32_ref, step))
        pair_out_ref[step] = values
        normed_ref[step] = layer_norm(values, 0).astype(BF16)
    project_out(
        normed_ref, weight, length, place_ref[0], place_ref[1], spread_ref, stage_ref, out_ref, out_sems
    )


def finish_kernel(recv_ref, pair_ref, gate_ref, out_weight_ref, out_ref, recv_f32_ref, stage_ref, sems):
    load_summed(recv_ref, recv_f32_ref)
    copies = []
    for part in range(4):
        for step in range(part * 4, part * 4 + 4):
            normed = normed_sum(recv_f32_ref, step).astype(F32)
            update = dot(jnp.transpose(normed, (1, 0)).astype(BF16), out_weight_ref[1])
            values = pair_step(pair_ref, step) + pair_step(gate_ref, step) * update
            stage_ref[:, step] = values.reshape(2, COLS, C)
        steps = pl.ds(part * 4, 4)
        copies.append(
            pltpu.make_async_copy(stage_ref.at[:, steps], out_ref.at[:, steps], sems.at[part])
        )
        copies[-1].start()
    for copy in copies:
        copy.wait()


def fence_kernel(*refs):
    refs[-1][...] = jnp.zeros_like(refs[-1])


def bias_kernel(prev_ref, weight_ref, *refs):
    out_ref, spread_ref = refs[-2:]

    def body(step, carry):
        normed = layer_norm(pair_step(prev_ref, step)).astype(BF16)
        spread_ref[pl.ds(step, HEADS, stride=16), :] = dot(weight_ref[...], normed, NT)
        return carry

    lax.fori_loop(0, 16, body, 0, unroll=4)
    out_ref[...] = spread_ref[...].astype(BF16).reshape(HEADS, 16, 128)


def copy_all(pairs, sems):
    copies = [
        pltpu.make_async_copy(source, dest, sems.at[index]) for index, (source, dest) in enumerate(pairs)
    ]
    for copy in copies:
        copy.start()
    return copies


def wait_all(copies):
    for copy in copies:
        copy.wait()


def tokens_kernel(
    place_ref, tokens_ref, atoms_ref, ids_ref, atom_weight_ref, weight_ref, *refs,
):
    start_out, gate_out, *sends = refs[-14:-4]
    start_ref, gate_ref, parts_ref, sems = refs[-4:]
    tokens, atoms = 64, 256
    local = ids_ref[...] - place_ref[1]
    onehot = (lax.broadcasted_iota(jnp.int32, (tokens, atoms), 0) == local).astype(F32)
    count = jnp.sum(onehot, axis=1, keepdims=True)
    onehot = onehot.astype(BF16)
    pooled = [(dot(onehot, atoms_ref[sample]) / count).astype(BF16) for sample in range(2)]
    start = tokens_ref[...].reshape(128, WIDTH) + dot(
        jnp.concatenate(pooled, axis=0), atom_weight_ref[...]
    )
    start_ref[...] = start
    normed = layer_norm(start).astype(BF16)
    for part in range(3):
        projected = dot(normed, weight_ref[:, part * WIDTH : (part + 1) * WIDTH])
        turned = jnp.transpose(projected, (1, 0)).astype(BF16)
        parts_ref[:, part * PAIR : (part + 1) * PAIR, :] = turned.reshape(8, PAIR, 128)
    copies = copy_all(
        [(parts_ref.at[place_ref[3] ^ slot], sends[slot]) for slot in range(8)] + [(start_ref, start_out)],
        sems,
    )
    gate_ref[...] = jax.nn.sigmoid(dot(normed, weight_ref[:, 3 * WIDTH :]))
    copies.append(pltpu.make_async_copy(gate_ref, gate_out, sems.at[9]))
    copies[-1].start()
    wait_all(copies)


def attention_kernel(place_ref, mask_ref, bias_ref, other_bias_ref, *refs):
    received, sends = refs[:8], refs[8:16]
    recv_ref, query_key_ref, value_ref, full_bias_ref, mixed_ref, out_ref, sems = refs[16:]
    own = place_ref[2]
    copies = copy_all(
        [(received[slot], recv_ref.at[place_ref[3] ^ slot]) for slot in range(8)], sems
    )
    live = lax.broadcasted_iota(jnp.int32, (1, TOK), 1) < mask_length(mask_ref)
    for block in range(4):
        lanes = slice(block * 128, (block + 1) * 128)
        for core, source_ref, base in ((own, bias_ref, 32), (1 - own, other_bias_ref, 0)):
            for head in range(2):
                rows = slice(base + 16 * head, base + 16 * head + 16)
                first, second = swap_halves(
                    source_ref[:, 2 * block, rows, :].astype(F32),
                    source_ref[:, 2 * block + 1, rows, :].astype(F32),
                )
                full_bias_ref[head, :, core, 0, :, lanes] = first.astype(BF16)
                full_bias_ref[head, :, core, 1, :, lanes] = second.astype(BF16)
    wait_all(copies)
    for block in range(4):
        lanes = slice(block * 128, (block + 1) * 128)
        halves = swap_halves(recv_ref[2 * block].astype(F32), recv_ref[2 * block + 1].astype(F32))
        for sample in range(2):
            half = halves[sample].astype(BF16)
            query_key_ref[sample, :, lanes] = half[: 2 * PAIR]
            for head in range(2):
                at = 2 * PAIR + head * HEAD
                value_ref[sample, head, :HEAD, lanes] = half[at : at + HEAD]
    value_ref[:, :, HEAD:, :] = jnp.ones((2, 2, 16, TOK), BF16)
    for head in range(2):
        bias = full_bias_ref[head].reshape(TOK, TOK)
        for sample in range(2):
            query = query_key_ref[sample, head * HEAD : (head + 1) * HEAD, :]
            key = query_key_ref[sample, PAIR + head * HEAD : PAIR + (head + 1) * HEAD, :]
            scores = dot(query, key, TN) * (HEAD**-0.5) + bias.astype(F32)
            scores = jnp.where(live, scores, -1e30)
            top = jnp.max(scores, axis=1, keepdims=True)
            weights = jnp.exp(scores - top).astype(BF16)
            mixed = dot(value_ref[sample, head], weights, NT)
            mixed_ref[sample, head * HEAD : (head + 1) * HEAD] = mixed[:HEAD] / mixed[HEAD : HEAD + 1]
    for block in range(4):
        lanes = slice(block * 128, (block + 1) * 128)
        first, second = swap_halves(mixed_ref[0, :, lanes], mixed_ref[1, :, lanes])
        out_ref[2 * block] = first.astype(BF16)
        out_ref[2 * block + 1] = second.astype(BF16)
    wait_all(copy_all([(out_ref.at[place_ref[3] ^ slot], sends[slot]) for slot in range(8)], sems))


def tokens_out_kernel(place_ref, gate_in, start_in, weight_in, *refs):
    received = refs[:8]
    out_ref, gate_ref, start_ref, weight_ref, recv_ref, sems = refs[8:]
    wait_all(
        copy_all(
            [(received[slot], recv_ref.at[place_ref[3] ^ slot]) for slot in range(8)]
            + [(gate_in, gate_ref), (start_in, start_ref), (weight_in, weight_ref)],
            sems,
        )
    )
    mixed = jnp.transpose(recv_ref[...].reshape(WIDTH, 128).astype(F32), (1, 0))
    blended = (gate_ref[...] * mixed).astype(BF16)
    out_ref[...] = (start_ref[...] + dot(blended, weight_ref[...])).reshape(2, 64, WIDTH)


def call(
    kernel, name, out_shape, scratch, *operands, smem=0, after=(), far=(), far_out=(), flops=10**8, limit=WIDE
):
    shapes = jax.tree.leaves(out_shape)
    nbytes = sum(v.size * v.dtype.itemsize for v in (*operands, *shapes))
    near = pl.BlockSpec(memory_space=pltpu.VMEM)
    anywhere = pl.BlockSpec(memory_space=pltpu.HBM)
    scalar = pl.BlockSpec(memory_space=pltpu.SMEM)
    outs = [anywhere if index in far_out else near for index in range(len(shapes))]
    return pl.pallas_call(
        kernel,
        name=name,
        out_shape=out_shape,
        in_specs=[
            scalar if index < smem else anywhere if index in far else near
            for index in range(len(operands))
        ]
        + [anywhere] * len(after),
        out_specs=outs if isinstance(out_shape, (list, tuple)) else outs[0],
        scratch_shapes=scratch,
        cost_estimate=pl.CostEstimate(flops=flops, bytes_accessed=nbytes, transcendentals=0),
        compiler_params=pltpu.CompilerParams(vmem_limit_bytes=limit),
    )(*operands, *after)


def shape(*dims, dtype=F32):
    return jax.ShapeDtypeStruct(dims, dtype)


ALL = ("z", "col")
EARLY, LATE = 1, 6


def from_other_core(value):
    return lax.ppermute(value, "core", [(0, 1), (1, 0)])


def exchange(value):
    return lax.all_to_all(value, ALL, 0, 0, tiled=True)


def swap(values, axis):
    return [values[0]] + [
        lax.ppermute(values[slot], axis, [(at, at ^ slot) for at in range(8)]) for slot in range(1, 8)
    ]


def on_device(
    pair, pair_mask, prev_pair, diff_tokens, diff_mask, atom_feats, atom_token,
    trunk_in, trunk_out, bias_weight, atom_weight, attn_in, attn_out,
):
    z, core, col = lax.axis_index("z"), lax.axis_index("core"), lax.axis_index("col")
    place = jnp.stack([(z * 2 + core) * ROWS, col * COLS, core, col, z]).astype(jnp.int32)
    tile = (2, 16, COLS, C)
    send = shape(C, 32, 128, dtype=BF16)
    normed = pltpu.VMEM((16, C, 128), BF16)
    spread = pltpu.VMEM((C * PITCH, 128), F32)
    stage = pltpu.VMEM((C, 32, 128), BF16)
    received = pltpu.VMEM((C * RECV_PITCH, 128), F32)
    half = pltpu.VMEM((2, 8, 2, 16, TOK), BF16)
    sums = shape(8, 8, 32, 128, dtype=BF16)
    sems = pltpu.SemaphoreType.DMA((4,))

    turned_tile = shape(16, C, 128)
    token_shape = shape(8, 128)

    pair0 = pair.reshape(tile)
    operands = call(
        project_kernel, "project", send,
        [
            pltpu.VMEM((1, TOK), jnp.int32), pltpu.VMEM(tile, F32), pltpu.VMEM((2, C, 5 * C), BF16),
            normed, spread, stage, pltpu.SemaphoreType.DMA((6,)), sems,
        ],
        place, pair_mask, pair0, trunk_in, smem=1, far=(1, 2, 3), far_out=(0,),
    )
    gathered = exchange(operands.reshape(64, 64, 128)).reshape(8, 8, 2, 32, 128)

    start, gate2, *parts = call(
        tokens_kernel, "tokens_in",
        [shape(128, WIDTH), shape(128, WIDTH)] + [shape(3 * PAIR, 128, dtype=BF16)] * 8,
        [
            pltpu.VMEM((128, WIDTH), F32), pltpu.VMEM((128, WIDTH), F32),
            pltpu.VMEM((8, 3 * PAIR, 128), BF16), pltpu.SemaphoreType.DMA((10,)),
        ],
        place, diff_tokens[0], atom_feats[0], atom_token, atom_weight, attn_in,
        smem=1, far_out=range(10), after=(operands,),
    )
    parts = swap(parts, "col")
    bias_here = call(
        bias_kernel, "bias", shape(HEADS, 16, 128, dtype=BF16), [pltpu.VMEM((HEADS * 16, 128), F32)],
        prev_pair.reshape(tile), jnp.swapaxes(bias_weight, 0, 1), after=(parts[0],),
    )
    bias_other = lax.ppermute(bias_here, "grp", [(0, 1), (1, 0)])

    right = call(
        take_right_kernel, "take_right", shape(8, 8, 2, 16, 128, dtype=BF16), [],
        gathered, bias_other, limit=NARROW,
    )
    summed0 = call(
        outgoing_kernel, "outgoing", shape(8, 8, 64, 128, dtype=BF16),
        [half, pltpu.VMEM((2, 8, 2, 2, 16, TOK), BF16)],
        place, gathered, from_other_core(right), bias_other,
        smem=1, flops=2 * TOK**3, limit=NARROW,
    )
    summed0 = exchange(summed0.reshape(64, 64, 128))
    token = call(fence_kernel, "fence", token_shape, [], after=tuple(parts[EARLY:]))
    pair0 = call(turn_kernel, "turn", turned_tile, [], pair0, after=(token,), limit=NARROW)

    pair1, operands = call(
        finish_project_kernel, "finish_project", (turned_tile, send), [received, normed, spread, stage, sems],
        place, pair_mask, summed0, pair0, trunk_out, trunk_in,
        smem=1, far_out=(1,), limit=FINISH,
    )
    gathered = exchange(operands.reshape(64, 64, 128)).reshape(8, 8, 2, 32, 128)
    bias_far = from_other_core(summed0[:, 32:, :])
    mixed = call(
        attention_kernel, "attention", [shape(PAIR, 128, dtype=BF16)] * 8,
        [
            pltpu.VMEM((8, 3 * PAIR, 128), BF16),
            pltpu.VMEM((2, 2 * PAIR, TOK), BF16),
            pltpu.VMEM((2, 2, HEAD + 16, TOK), BF16),
            pltpu.VMEM((2, 8, 2, 2, 16, TOK), BF16),
            pltpu.VMEM((2, PAIR, TOK), F32),
            pltpu.VMEM((8, PAIR, 128), BF16),
            pltpu.SemaphoreType.DMA((8,)),
        ],
        place, diff_mask, summed0.reshape(8, 8, 64, 128), bias_far.reshape(8, 8, 32, 128), *parts,
        smem=1, far=range(4, 12), far_out=range(8),
    )
    mixed = swap(mixed, "col")
    token = call(fence_kernel, "fence", token_shape, [], after=tuple(mixed[1:LATE]))
    own, far = call(
        incoming_kernel, "incoming", [sums, sums], [half, half],
        place, gathered, token, smem=1, flops=2 * TOK**3, limit=NARROW,
    )
    summed1 = call(add_kernel, "add", sums, [], own, from_other_core(far), limit=NARROW)
    summed1 = exchange(summed1.reshape(64, 32, 128))
    tokens_done = call(
        tokens_out_kernel, "tokens_out", shape(2, 64, WIDTH),
        [
            pltpu.VMEM((128, WIDTH), F32), pltpu.VMEM((128, WIDTH), F32), pltpu.VMEM((WIDTH, WIDTH), BF16),
            pltpu.VMEM((8, PAIR, 128), BF16), pltpu.SemaphoreType.DMA((11,)),
        ],
        place, gate2, start, attn_out, *mixed, smem=1, far=range(1, 12),
    )
    pair1, gate1 = call(
        gate_back_kernel, "gate_back", [shape(*tile), shape(*tile)], [], pair1, trunk_in,
        limit=MIDDLE,
    )
    pair2 = call(
        finish_kernel, "finish", shape(*tile), [received, pltpu.VMEM(tile, F32), sems],
        summed1, pair1, gate1, trunk_out, far_out=(0,), limit=NARROW,
    )
    return (pair2.reshape(1, ROWS, COLS, C), tokens_done[None])


def solution(mesh):
    split = Mesh(mesh.devices.reshape(2, 8, 2, 8), ("grp", "z", "core", "col"))
    row = ("z", "core")
    placed = (
        P("grp", row, "col", None),
        P("grp", None),
        P("grp", row, "col", None),
        P("grp", row, "col", None),
        P("grp", None),
        P("grp", row, "col", None),
        P("grp", "col"),
        P(),
        P(),
        P(),
        P(),
        P(),
        P(),
    )
    return jax.shard_map(
        on_device,
        mesh=split,
        in_specs=placed,
        out_specs=(P("grp", row, "col", None), P("grp", row, "col", None)),
        check_vma=False,
    )
```

```python
import functools

import jax
import jax.numpy as jnp
from jax import lax
from jax.experimental import pallas as pl
from jax.experimental.pallas import tpu as pltpu
from jax.sharding import Mesh, PartitionSpec as P

EPSILON = 1e-05
F32, BF16 = jnp.float32, jnp.bfloat16
ROWS, COLS, TOK, C = 32, 64, 512, 128
HEADS, HEAD = 16, 48
WIDTH, PAIR = HEADS * HEAD, 2 * HEAD
WIDE, MIDDLE, NARROW = 63_000_000, 40_000_000, 24 * 2**20
FINISH = 24 * 2**20
PITCH, RECV_PITCH = 40, 24
NT = (((1,), (1,)), ((), ()))
TN = (((0,), (0,)), ((), ()))


def dot(left, right, dims=(((1,), (0,)), ((), ()))):
    return lax.dot_general(left, right, dims, preferred_element_type=F32)


def layer_norm(values, axis=-1):
    centred = values - jnp.mean(values, axis=axis, keepdims=True)
    spread = jnp.mean(centred * centred, axis=axis, keepdims=True)
    return centred * lax.rsqrt(spread + EPSILON)


def low_lanes():
    return lax.broadcasted_iota(jnp.int32, (1, 128), 1) < 64


def swap_halves(first, second):
    low = low_lanes()
    axis = first.ndim - 1
    return (
        jnp.where(low, first, pltpu.roll(second, 64, axis)),
        jnp.where(low, pltpu.roll(first, 64, axis), second),
    )


def pair_step(pair_ref, step):
    return pair_ref[:, step].reshape(2 * COLS, C)


def turned(weight):
    return jnp.transpose(weight.astype(F32), (1, 0)).astype(BF16)


def quarter_weight(weight):
    return turned(weight).reshape(4, 4, 32, C)


def project_out(normed_ref, weight, length, row0, col0, spread_ref, stage_ref, out_ref, sems):
    lane = lax.broadcasted_iota(jnp.int32, (1, 128), 1)
    half = (lane >= 64).astype(jnp.int32)
    col_live = col0 + lane - half * 64 < length
    copies = []
    for quarter in range(4):
        part_weight = jnp.concatenate([weight[part, quarter] for part in range(4)], axis=0)
        base = quarter * 32 * PITCH
        for step in range(16):
            live = jnp.logical_and(row0 + half * 16 + step < length, col_live).astype(F32)
            projected = dot(part_weight, normed_ref[step])
            left = live * jax.nn.sigmoid(projected[:32]) * projected[32:64]
            right = live * jax.nn.sigmoid(projected[64:96]) * projected[96:]
            spread_ref[pl.ds(base + step, 32, stride=PITCH), :] = left
            spread_ref[pl.ds(base + step + 16, 32, stride=PITCH), :] = right
        chunk = pl.ds(quarter * 32, 32)
        values = spread_ref[pl.ds(base, 32 * PITCH), :].reshape(32, PITCH, 128)
        stage_ref[chunk] = values[:, :32].astype(BF16)
        copies.append(pltpu.make_async_copy(stage_ref.at[chunk], out_ref.at[chunk], sems.at[quarter]))
        copies[-1].start()
    for copy in copies:
        copy.wait()


def mask_length(mask_ref):
    return jnp.sum(mask_ref[...])


def project_kernel(
    mask_in, pair_in, weight_in, out_ref,
    mask_ref, pair_ref, weight_ref, normed_ref, spread_ref, stage_ref, in_sems, out_sems,
):
    row0 = (lax.axis_index("z") * 2 + lax.axis_index("core")) * ROWS
    col0 = lax.axis_index("col") * COLS
    copies = [
        pltpu.make_async_copy(mask_in, mask_ref, in_sems.at[4]),
        pltpu.make_async_copy(weight_in, weight_ref, in_sems.at[5]),
    ]
    for part in range(4):
        steps = pl.ds(part * 4, 4)
        copies.append(
            pltpu.make_async_copy(pair_in.at[:, steps], pair_ref.at[:, steps], in_sems.at[part])
        )
    for copy in copies:
        copy.start()
    copies[0].wait()
    copies[1].wait()
    length = mask_length(mask_ref)
    weight = quarter_weight(weight_ref[0, :, : 4 * C])
    for part in range(4):
        copies[2 + part].wait()
        for step in range(part * 4, part * 4 + 4):
            values = jnp.transpose(pair_step(pair_ref, step), (1, 0))
            normed_ref[step] = layer_norm(values, 0).astype(BF16)
    project_out(
        normed_ref, weight, length, row0, col0, spread_ref, stage_ref, out_ref, out_sems
    )


def turn_kernel(pair_ref, *refs):
    for step in range(16):
        refs[-1][step] = jnp.transpose(pair_step(pair_ref, step), (1, 0))


def gate_back_kernel(pair_ref, weight_ref, *refs):
    pair_out_ref, gate_ref = refs[-2:]
    weight = turned(weight_ref[1, :, 4 * C :])
    for step in range(16):
        values = pair_ref[step]
        gate = jax.nn.sigmoid(dot(weight, layer_norm(values, 0).astype(BF16)))
        pair_out_ref[:, step] = jnp.transpose(values, (1, 0)).reshape(2, COLS, C)
        gate_ref[:, step] = jnp.transpose(gate, (1, 0)).reshape(2, COLS, C)


def tiles_to_rows(recv_ref, rows, channel, dest):
    for block in range(4):
        lanes = slice(block * 128, (block + 1) * 128)
        halves = swap_halves(
            recv_ref[:, 2 * block, channel, rows, :].astype(F32),
            recv_ref[:, 2 * block + 1, channel, rows, :].astype(F32),
        )
        for half in range(2):
            ref, index = dest(half, lanes)
            ref[index] = halves[half].astype(BF16)


def outgoing_kernel(place_ref, recv_ref, far_ref, bias_ref, out_ref, left_ref, right_ref):
    own = place_ref[2]
    for head in range(2):
        for col in range(8):
            tile = bias_ref[2 * col + head]
            rows = slice(32 + 16 * head, 48 + 16 * head)
            out_ref[:, col, rows, :] = jnp.broadcast_to(tile[None], (8, 16, 128))
    for channel in range(2):
        tiles_to_rows(
            recv_ref, slice(16), channel,
            lambda half, lanes: (left_ref, (channel, slice(None), half, slice(None), lanes)),
        )
        for core, ref, rows in ((own, recv_ref, slice(16, 32)), (1 - own, far_ref, slice(16))):
            tiles_to_rows(
                ref, rows, channel,
                lambda half, lanes: (right_ref, (channel, slice(None), core, half, slice(None), lanes)),
            )
        left = left_ref[channel].reshape(TOK // 2, TOK)
        right = right_ref[channel].reshape(TOK, TOK)
        rows = slice(16 * channel, 16 * channel + 16)
        for block in range(4):
            summed = dot(left, right[block * 128 : (block + 1) * 128], NT).reshape(8, 2, 16, 128)
            first, second = swap_halves(summed[:, 0], summed[:, 1])
            out_ref[:, 2 * block, rows, :] = first.astype(BF16)
            out_ref[:, 2 * block + 1, rows, :] = second.astype(BF16)


def take_right_kernel(recv_ref, bias_ref, out_ref):
    out_ref[...] = recv_ref[:, :, :, 16:, :]


def incoming_kernel(place_ref, recv_ref, token_ref, own_ref, far_ref, left_ref, right_ref):
    first_core = place_ref[2] == 0
    for channel in range(2):
        for ref, rows in ((left_ref, slice(16)), (right_ref, slice(16, 32))):
            tiles_to_rows(
                recv_ref, rows, channel,
                lambda half, lanes: (ref, (channel, slice(None), half, slice(None), lanes)),
            )
        left = left_ref[channel].reshape(TOK // 2, TOK)
        right = right_ref[channel].reshape(TOK // 2, TOK)
        rows = slice(16 * channel, 16 * channel + 16)
        for block in range(4):
            summed = dot(left, right[:, block * 128 : (block + 1) * 128], TN).reshape(8, 2, 2, 16, 128)
            for out_ref, kept in (
                (own_ref, jnp.where(first_core, summed[:, 0], summed[:, 1])),
                (far_ref, jnp.where(first_core, summed[:, 1], summed[:, 0])),
            ):
                first, second = swap_halves(kept[:, 0], kept[:, 1])
                out_ref[:, 2 * block, rows, :] = first.astype(BF16)
                out_ref[:, 2 * block + 1, rows, :] = second.astype(BF16)


def add_kernel(own_ref, far_ref, out_ref):
    out_ref[...] = (own_ref[...].astype(F32) + far_ref[...].astype(F32)).astype(BF16)


def load_summed(recv_ref, recv_f32_ref):
    recv_f32_ref.reshape(C, RECV_PITCH, 128)[:, :16] = recv_ref[:, :32, :].reshape(C, 16, 128).astype(F32)


def normed_sum(recv_f32_ref, step):
    return layer_norm(recv_f32_ref[pl.ds(step, C, stride=RECV_PITCH), :], 0).astype(BF16)


def finish_project_kernel(
    place_ref, mask_ref, recv_ref, pair_ref, out_weight_ref, in_weight_ref,
    pair_out_ref, out_ref, recv_f32_ref, normed_ref, spread_ref, stage_ref, out_sems,
):
    length = mask_length(mask_ref)
    weight = quarter_weight(in_weight_ref[1, :, : 4 * C])
    gate_weight = turned(in_weight_ref[0, :, 4 * C :])
    out_weight = turned(out_weight_ref[0])
    load_summed(recv_ref, recv_f32_ref)
    for step in range(16):
        values = pair_ref[step]
        gate = jax.nn.sigmoid(dot(gate_weight, layer_norm(values, 0).astype(BF16)))
        values = values + gate * dot(out_weight, normed_sum(recv_f32_ref, step))
        pair_out_ref[step] = values
        normed_ref[step] = layer_norm(values, 0).astype(BF16)
    project_out(
        normed_ref, weight, length, place_ref[0], place_ref[1], spread_ref, stage_ref, out_ref, out_sems
    )


def finish_kernel(recv_ref, pair_ref, gate_ref, out_weight_ref, out_ref, recv_f32_ref, stage_ref, sems):
    load_summed(recv_ref, recv_f32_ref)
    copies = []
    for part in range(4):
        for step in range(part * 4, part * 4 + 4):
            normed = normed_sum(recv_f32_ref, step).astype(F32)
            update = dot(jnp.transpose(normed, (1, 0)).astype(BF16), out_weight_ref[1])
            values = pair_step(pair_ref, step) + pair_step(gate_ref, step) * update
            stage_ref[:, step] = values.reshape(2, COLS, C)
        steps = pl.ds(part * 4, 4)
        copies.append(
            pltpu.make_async_copy(stage_ref.at[:, steps], out_ref.at[:, steps], sems.at[part])
        )
        copies[-1].start()
    for copy in copies:
        copy.wait()


def fence_kernel(*refs):
    refs[-1][...] = jnp.zeros_like(refs[-1])


def bias_kernel(prev_ref, weight_ref, *refs):
    out_ref, spread_ref = refs[-2:]

    def body(step, carry):
        normed = layer_norm(pair_step(prev_ref, step)).astype(BF16)
        spread_ref[pl.ds(step, HEADS, stride=16), :] = dot(weight_ref[...], normed, NT)
        return carry

    lax.fori_loop(0, 16, body, 0, unroll=4)
    out_ref[...] = spread_ref[...].astype(BF16).reshape(HEADS, 16, 128)


def copy_all(pairs, sems):
    copies = [
        pltpu.make_async_copy(source, dest, sems.at[index]) for index, (source, dest) in enumerate(pairs)
    ]
    for copy in copies:
        copy.start()
    return copies


def wait_all(copies):
    for copy in copies:
        copy.wait()


def tokens_kernel(
    place_ref, tokens_ref, atoms_ref, ids_ref, atom_weight_ref, weight_ref, *refs,
):
    start_out, gate_out, *sends = refs[-14:-4]
    start_ref, gate_ref, parts_ref, sems = refs[-4:]
    tokens, atoms = 64, 256
    local = ids_ref[...] - place_ref[1]
    onehot = (lax.broadcasted_iota(jnp.int32, (tokens, atoms), 0) == local).astype(F32)
    count = jnp.sum(onehot, axis=1, keepdims=True)
    onehot = onehot.astype(BF16)
    pooled = [(dot(onehot, atoms_ref[sample]) / count).astype(BF16) for sample in range(2)]
    start = tokens_ref[...].reshape(128, WIDTH) + dot(
        jnp.concatenate(pooled, axis=0), atom_weight_ref[...]
    )
    start_ref[...] = start
    normed = layer_norm(start).astype(BF16)
    for part in range(3):
        projected = dot(normed, weight_ref[:, part * WIDTH : (part + 1) * WIDTH])
        turned = jnp.transpose(projected, (1, 0)).astype(BF16)
        parts_ref[:, part * PAIR : (part + 1) * PAIR, :] = turned.reshape(8, PAIR, 128)
    copies = copy_all(
        [(parts_ref.at[place_ref[3] ^ slot], sends[slot]) for slot in range(8)] + [(start_ref, start_out)],
        sems,
    )
    gate_ref[...] = jax.nn.sigmoid(dot(normed, weight_ref[:, 3 * WIDTH :]))
    copies.append(pltpu.make_async_copy(gate_ref, gate_out, sems.at[9]))
    copies[-1].start()
    wait_all(copies)


def attention_kernel(place_ref, mask_ref, bias_ref, other_bias_ref, *refs):
    received, sends = refs[:8], refs[8:16]
    recv_ref, query_key_ref, value_ref, full_bias_ref, mixed_ref, out_ref, sems = refs[16:]
    own = place_ref[2]
    copies = copy_all(
        [(received[slot], recv_ref.at[place_ref[3] ^ slot]) for slot in range(8)], sems
    )
    live = lax.broadcasted_iota(jnp.int32, (1, TOK), 1) < mask_length(mask_ref)
    for block in range(4):
        lanes = slice(block * 128, (block + 1) * 128)
        for core, source_ref, base in ((own, bias_ref, 32), (1 - own, other_bias_ref, 0)):
            for head in range(2):
                rows = slice(base + 16 * head, base + 16 * head + 16)
                first, second = swap_halves(
                    source_ref[:, 2 * block, rows, :].astype(F32),
                    source_ref[:, 2 * block + 1, rows, :].astype(F32),
                )
                full_bias_ref[head, :, core, 0, :, lanes] = first.astype(BF16)
                full_bias_ref[head, :, core, 1, :, lanes] = second.astype(BF16)
    wait_all(copies)
    for block in range(4):
        lanes = slice(block * 128, (block + 1) * 128)
        halves = swap_halves(recv_ref[2 * block].astype(F32), recv_ref[2 * block + 1].astype(F32))
        for sample in range(2):
            half = halves[sample].astype(BF16)
            query_key_ref[sample, :, lanes] = half[: 2 * PAIR]
            for head in range(2):
                at = 2 * PAIR + head * HEAD
                value_ref[sample, head, :HEAD, lanes] = half[at : at + HEAD]
    value_ref[:, :, HEAD:, :] = jnp.ones((2, 2, 16, TOK), BF16)
    for head in range(2):
        bias = full_bias_ref[head].reshape(TOK, TOK)
        for sample in range(2):
            query = query_key_ref[sample, head * HEAD : (head + 1) * HEAD, :]
            key = query_key_ref[sample, PAIR + head * HEAD : PAIR + (head + 1) * HEAD, :]
            scores = dot(query, key, TN) * (HEAD**-0.5) + bias.astype(F32)
            scores = jnp.where(live, scores, -1e30)
            top = jnp.max(scores, axis=1, keepdims=True)
            weights = jnp.exp(scores - top).astype(BF16)
            mixed = dot(value_ref[sample, head], weights, NT)
            mixed_ref[sample, head * HEAD : (head + 1) * HEAD] = mixed[:HEAD] / mixed[HEAD : HEAD + 1]
    for block in range(4):
        lanes = slice(block * 128, (block + 1) * 128)
        first, second = swap_halves(mixed_ref[0, :, lanes], mixed_ref[1, :, lanes])
        out_ref[2 * block] = first.astype(BF16)
        out_ref[2 * block + 1] = second.astype(BF16)
    wait_all(copy_all([(out_ref.at[place_ref[3] ^ slot], sends[slot]) for slot in range(8)], sems))


def tokens_out_kernel(place_ref, gate_in, start_in, weight_in, *refs):
    received = refs[:8]
    out_ref, gate_ref, start_ref, weight_ref, recv_ref, sems = refs[8:]
    wait_all(
        copy_all(
            [(received[slot], recv_ref.at[place_ref[3] ^ slot]) for slot in range(8)]
            + [(gate_in, gate_ref), (start_in, start_ref), (weight_in, weight_ref)],
            sems,
        )
    )
    mixed = jnp.transpose(recv_ref[...].reshape(WIDTH, 128).astype(F32), (1, 0))
    blended = (gate_ref[...] * mixed).astype(BF16)
    out_ref[...] = (start_ref[...] + dot(blended, weight_ref[...])).reshape(2, 64, WIDTH)


def call(
    kernel, name, out_shape, scratch, *operands, smem=0, after=(), far=(), far_out=(), flops=10**8, limit=WIDE
):
    shapes = jax.tree.leaves(out_shape)
    nbytes = sum(v.size * v.dtype.itemsize for v in (*operands, *shapes))
    near = pl.BlockSpec(memory_space=pltpu.VMEM)
    anywhere = pl.BlockSpec(memory_space=pltpu.HBM)
    scalar = pl.BlockSpec(memory_space=pltpu.SMEM)
    outs = [anywhere if index in far_out else near for index in range(len(shapes))]
    return pl.pallas_call(
        kernel,
        name=name,
        out_shape=out_shape,
        in_specs=[
            scalar if index < smem else anywhere if index in far else near
            for index in range(len(operands))
        ]
        + [anywhere] * len(after),
        out_specs=outs if isinstance(out_shape, (list, tuple)) else outs[0],
        scratch_shapes=scratch,
        cost_estimate=pl.CostEstimate(flops=flops, bytes_accessed=nbytes, transcendentals=0),
        compiler_params=pltpu.CompilerParams(vmem_limit_bytes=limit),
    )(*operands, *after)


def shape(*dims, dtype=F32):
    return jax.ShapeDtypeStruct(dims, dtype)


ALL = ("z", "col")
EARLY, LATE = 1, 6


def from_other_core(value):
    return lax.ppermute(value, "core", [(0, 1), (1, 0)])


def exchange(value):
    return lax.all_to_all(value, ALL, 0, 0, tiled=True)


def swap(values, axis):
    return [values[0]] + [
        lax.ppermute(values[slot], axis, [(at, at ^ slot) for at in range(8)]) for slot in range(1, 8)
    ]


def on_device(
    pair, pair_mask, prev_pair, diff_tokens, diff_mask, atom_feats, atom_token,
    trunk_in, trunk_out, bias_weight, atom_weight, attn_in, attn_out,
):
    z, core, col = lax.axis_index("z"), lax.axis_index("core"), lax.axis_index("col")
    place = jnp.stack([(z * 2 + core) * ROWS, col * COLS, core, col, z]).astype(jnp.int32)
    tile = (2, 16, COLS, C)
    send = shape(C, 32, 128, dtype=BF16)
    normed = pltpu.VMEM((16, C, 128), BF16)
    spread = pltpu.VMEM((C * PITCH, 128), F32)
    stage = pltpu.VMEM((C, 32, 128), BF16)
    received = pltpu.VMEM((C * RECV_PITCH, 128), F32)
    half = pltpu.VMEM((2, 8, 2, 16, TOK), BF16)
    sums = shape(8, 8, 32, 128, dtype=BF16)
    sems = pltpu.SemaphoreType.DMA((4,))

    turned_tile = shape(16, C, 128)
    token_shape = shape(8, 128)

    pair0 = pair.reshape(tile)
    operands = call(
        project_kernel, "project", send,
        [
            pltpu.VMEM((1, TOK), jnp.int32), pltpu.VMEM(tile, F32), pltpu.VMEM((2, C, 5 * C), BF16),
            normed, spread, stage, pltpu.SemaphoreType.DMA((6,)), sems,
        ],
        pair_mask, pair0, trunk_in, far=(0, 1, 2), far_out=(0,),
    )
    gathered = exchange(operands.reshape(64, 64, 128)).reshape(8, 8, 2, 32, 128)

    start, gate2, *parts = call(
        tokens_kernel, "tokens_in",
        [shape(128, WIDTH), shape(128, WIDTH)] + [shape(3 * PAIR, 128, dtype=BF16)] * 8,
        [
            pltpu.VMEM((128, WIDTH), F32), pltpu.VMEM((128, WIDTH), F32),
            pltpu.VMEM((8, 3 * PAIR, 128), BF16), pltpu.SemaphoreType.DMA((10,)),
        ],
        place, diff_tokens[0], atom_feats[0], atom_token, atom_weight, attn_in,
        smem=1, far_out=range(10), after=(operands,),
    )
    parts = swap(parts, "col")
    bias_here = call(
        bias_kernel, "bias", shape(HEADS, 16, 128, dtype=BF16), [pltpu.VMEM((HEADS * 16, 128), F32)],
        prev_pair.reshape(tile), jnp.swapaxes(bias_weight, 0, 1), after=(parts[0],),
    )
    bias_other = lax.ppermute(bias_here, "grp", [(0, 1), (1, 0)])

    right = call(
        take_right_kernel, "take_right", shape(8, 8, 2, 16, 128, dtype=BF16), [],
        gathered, bias_other, limit=NARROW,
    )
    summed0 = call(
        outgoing_kernel, "outgoing", shape(8, 8, 64, 128, dtype=BF16),
        [half, pltpu.VMEM((2, 8, 2, 2, 16, TOK), BF16)],
        place, gathered, from_other_core(right), bias_other,
        smem=1, flops=2 * TOK**3, limit=NARROW,
    )
    summed0 = exchange(summed0.reshape(64, 64, 128))
    token = call(fence_kernel, "fence", token_shape, [], after=tuple(parts[EARLY:]))
    pair0 = call(turn_kernel, "turn", turned_tile, [], pair0, after=(token,), limit=NARROW)

    pair1, operands = call(
        finish_project_kernel, "finish_project", (turned_tile, send), [received, normed, spread, stage, sems],
        place, pair_mask, summed0, pair0, trunk_out, trunk_in,
        smem=1, far_out=(1,), limit=FINISH,
    )
    gathered = exchange(operands.reshape(64, 64, 128)).reshape(8, 8, 2, 32, 128)
    bias_far = from_other_core(summed0[:, 32:, :])
    mixed = call(
        attention_kernel, "attention", [shape(PAIR, 128, dtype=BF16)] * 8,
        [
            pltpu.VMEM((8, 3 * PAIR, 128), BF16),
            pltpu.VMEM((2, 2 * PAIR, TOK), BF16),
            pltpu.VMEM((2, 2, HEAD + 16, TOK), BF16),
            pltpu.VMEM((2, 8, 2, 2, 16, TOK), BF16),
            pltpu.VMEM((2, PAIR, TOK), F32),
            pltpu.VMEM((8, PAIR, 128), BF16),
            pltpu.SemaphoreType.DMA((8,)),
        ],
        place, diff_mask, summed0.reshape(8, 8, 64, 128), bias_far.reshape(8, 8, 32, 128), *parts,
        smem=1, far=range(4, 12), far_out=range(8),
    )
    mixed = swap(mixed, "col")
    token = call(fence_kernel, "fence", token_shape, [], after=tuple(mixed[1:LATE]))
    own, far = call(
        incoming_kernel, "incoming", [sums, sums], [half, half],
        place, gathered, token, smem=1, flops=2 * TOK**3, limit=NARROW,
    )
    summed1 = call(add_kernel, "add", sums, [], own, from_other_core(far), limit=NARROW)
    summed1 = exchange(summed1.reshape(64, 32, 128))
    tokens_done = call(
        tokens_out_kernel, "tokens_out", shape(2, 64, WIDTH),
        [
            pltpu.VMEM((128, WIDTH), F32), pltpu.VMEM((128, WIDTH), F32), pltpu.VMEM((WIDTH, WIDTH), BF16),
            pltpu.VMEM((8, PAIR, 128), BF16), pltpu.SemaphoreType.DMA((11,)),
        ],
        place, gate2, start, attn_out, *mixed, smem=1, far=range(1, 12),
    )
    pair1, gate1 = call(
        gate_back_kernel, "gate_back", [shape(*tile), shape(*tile)], [], pair1, trunk_in,
        limit=MIDDLE,
    )
    pair2 = call(
        finish_kernel, "finish", shape(*tile), [received, pltpu.VMEM(tile, F32), sems],
        summed1, pair1, gate1, trunk_out, far_out=(0,), limit=NARROW,
    )
    return (pair2.reshape(1, ROWS, COLS, C), tokens_done[None])


def solution(mesh):
    split = Mesh(mesh.devices.reshape(2, 8, 2, 8), ("grp", "z", "core", "col"))
    row = ("z", "core")
    placed = (
        P("grp", row, "col", None),
        P("grp", None),
        P("grp", row, "col", None),
        P("grp", row, "col", None),
        P("grp", None),
        P("grp", row, "col", None),
        P("grp", "col"),
        P(),
        P(),
        P(),
        P(),
        P(),
        P(),
    )
    return jax.shard_map(
        on_device,
        mesh=split,
        in_specs=placed,
        out_specs=(P("grp", row, "col", None), P("grp", row, "col", None)),
        check_vma=False,
    )
```
